256 devices in a mesh: list: 64 (over z_lo, y, x, core), row: 4 (over z_hi).
Axes of the slice: x: 4, y: 4, z: 8 (z_hi: 4, z_lo: 2; z = z_hi * 2 + z_lo), core: 2. Of those that a mesh axis runs over, the one named last changes fastest.
Arguments:
- corpus: bfloat16 [262144, 768], P(('list', 'row')), may hold values from -6 to 6
- row_list: int32 [262144], P(('list', 'row')), may hold values from 0 to 4095, as said below
- list_slot: int32 [4096], replicated, may hold values from 0 to 4095, as said below
- member_counts: int32 [4096], P('list'), may hold values from 32 to 96, as said below
- old_centroids: float32 [4096, 768], P('list'), may hold values from -6 to 6
- next_rows: bfloat16 [393216, 768], P(('list', 'row')), may hold values from -6 to 6
Outputs:
- new_centroids: float32 [4096, 768], P('list')
- best_score: float32 [393216], P(('list', 'row'))
The draws below stay inside these ranges and needn't reach their ends.
Inputs may be any that keep to these rules, and one draw needn't show every extreme that they name: `row_list`: each device sends every owner (list_slot // 64) at least 8 and at most 24 of its rows; some owner receives 24 rows from every device. `list_slot`: A permutation of the list numbers. `member_counts`: the exact number of corpus rows in each slot's list; the lists of one owner differ by at most one.
All inputs are finite; a program needn't handle non-finite values.
Results may differ from the reference program's by a relative error of at most 0.0025.
Values may be sent and summed in bfloat16 or wider, within the bound.
A program may use at most 64 MiB of HBM per device.

```python
import jax
import jax.numpy as jnp
from jax import lax

D = 768
LO = 64
ITERS = 3
ROW_DEV = 1024
NEXT_DEV = 1536
LISTS = 4096
ROWS = 262144
NEXT = 393216
N_LIST = 64
N_ROW = 4


def make_layout(key):
    n_blocks = N_LIST * N_ROW
    per_owner = ROW_DEV // N_LIST
    half_spread = per_owner // 2
    slot_of_list = jax.random.permutation(jax.random.fold_in(key, 11), LISTS).astype(jnp.int32)
    list_of_slot = jnp.argsort(slot_of_list).astype(jnp.int32)
    forced_one = jax.random.randint(jax.random.fold_in(key, 12), (), 0, N_LIST).astype(jnp.int32)
    pair_keys = jax.random.split(jax.random.fold_in(key, 13), n_blocks)
    pairing = jax.vmap(lambda sub_key: jax.random.permutation(sub_key, N_LIST))(pair_keys).astype(jnp.int32)
    shifts = jax.random.randint(jax.random.fold_in(key, 14), (n_blocks, N_LIST // 2), -half_spread, half_spread + 1).astype(jnp.int32)
    block_range = jnp.arange(n_blocks, dtype=jnp.int32)
    forced_block = jnp.zeros((n_blocks,), jnp.int32) + forced_one
    position = jnp.argmax((pairing == forced_block[:, None]).astype(jnp.int32), axis=1).astype(jnp.int32)
    signed = jnp.where(position % 2 == 0, half_spread, -half_spread).astype(jnp.int32)
    shifts = shifts.at[block_range, position // 2].set(signed)
    pos_counts = jnp.stack([per_owner + shifts, per_owner - shifts], axis=2).reshape(n_blocks, N_LIST)
    counts_bo = jnp.zeros((n_blocks, N_LIST), jnp.int32).at[block_range[:, None], pairing].set(pos_counts)
    ends = jnp.cumsum(counts_bo, axis=1).astype(jnp.int32)
    starts = ends - counts_bo
    owner_seq = jnp.sum((ends[:, None, :] <= jnp.arange(ROW_DEV, dtype=jnp.int32)[None, :, None]).astype(jnp.int32), axis=2)
    order_keys = jax.random.split(jax.random.fold_in(key, 15), n_blocks)
    order = jax.vmap(lambda sub_key: jax.random.permutation(sub_key, ROW_DEV))(order_keys).astype(jnp.int32)
    owner_row = jnp.take_along_axis(owner_seq, order, axis=1)
    rank_in = order - jnp.take_along_axis(starts, owner_row, axis=1)
    before = (jnp.cumsum(counts_bo, axis=0) - counts_bo).astype(jnp.int32)
    global_rank = rank_in + jnp.take_along_axis(before, owner_row, axis=1)
    offsets = jax.random.randint(jax.random.fold_in(key, 16), (N_LIST,), 0, LO).astype(jnp.int32)
    local_id = (global_rank + offsets[owner_row]) % LO
    slot_rows = (owner_row * LO + local_id).reshape(ROWS).astype(jnp.int32)
    row_ids = list_of_slot[slot_rows]
    counts_slot = jnp.zeros((LISTS,), jnp.int32).at[slot_rows].add(1)
    return (row_ids, slot_of_list, counts_slot)


def draw_row_list(key, part):
    return make_layout(key)[0]


def draw_list_slot(key, part):
    return make_layout(key)[1]


def draw_member_counts(key, part):
    return make_layout(key)[2]


def steps_of(own_key, shape, cuts, low, largest):
    loudness, own = 1.0, jax.random.fold_in(own_key, 6)
    for axis_at, shards_of in cuts:
        steps = jnp.exp(jax.random.uniform(jax.random.fold_in(own, axis_at), (shards_of,), jnp.float32, low / len(cuts), largest / len(cuts)))
        loudness = loudness * jnp.repeat(steps, shape[axis_at] // shards_of).reshape([-1 if axis == axis_at else 1 for axis in range(len(shape))])
    return loudness


def centred(own_key, shape, deviation, reach, cuts=(), kind=jnp.bfloat16):
    gain = steps_of(own_key, shape, cuts, -0.22, 0.18) if cuts else 1.0
    values = jax.random.normal(own_key, shape, jnp.float32) * deviation * gain
    return jnp.minimum(jnp.maximum(values, -reach), reach).astype(kind)


def setup_inputs(seed: int = 0) -> dict:
    keys = jax.random.split(jax.random.key(seed), 7)
    return {
        "corpus": centred(keys[0], (ROWS, D), 1.0, 6.0, ((0, 256),)),
        "row_list": draw_row_list(jax.random.fold_in(keys[6], 71), 0),
        "list_slot": draw_list_slot(jax.random.fold_in(keys[6], 71), 0),
        "member_counts": draw_member_counts(jax.random.fold_in(keys[6], 71), 0),
        "old_centroids": centred(keys[4], (LISTS, D), 1.0, 6.0, ((0, 64),), jnp.float32),
        "next_rows": centred(keys[5], (NEXT, D), 1.0, 6.0, ((0, 256),)),
    }


eps_norm = 1e-06
aniso_par = 32.0
perp_weight = 1.0
prior_weight = 16.0

def unit_of(row_block):
    values = row_block.astype(jnp.float32)
    scaled = values / jnp.sqrt(lax.optimization_barrier(jnp.sum(values * values, axis=1, keepdims=True)) + eps_norm)
    return lax.optimization_barrier(scaled.astype(jnp.bfloat16)).astype(jnp.float32)

def reference(corpus, row_list, list_slot, member_counts, old_centroids, next_rows):
    slot_ids = list_slot[row_list].astype(jnp.int32)
    n_blocks = ROWS // ROW_DEV

    def gram_all(vectors):

        def add_block(block_idx, total):
            row_block = lax.dynamic_slice_in_dim(corpus, block_idx * ROW_DEV, ROW_DEV, 0)
            block_ids = lax.dynamic_slice_in_dim(slot_ids, block_idx * ROW_DEV, ROW_DEV, 0)
            unit_rows = unit_of(row_block)
            along = lax.optimization_barrier(jnp.sum(unit_rows * vectors[block_ids], axis=1, keepdims=True))
            return total + jax.ops.segment_sum(unit_rows * along, block_ids, num_segments=LISTS)
        return lax.fori_loop(0, n_blocks, add_block, jnp.zeros((LISTS, D), jnp.float32))

    def add_rows(block_idx, total):
        row_block = lax.dynamic_slice_in_dim(corpus, block_idx * ROW_DEV, ROW_DEV, 0)
        block_ids = lax.dynamic_slice_in_dim(slot_ids, block_idx * ROW_DEV, ROW_DEV, 0)
        return total + jax.ops.segment_sum(row_block.astype(jnp.float32), block_ids, num_segments=LISTS)
    row_sums = lax.fori_loop(0, n_blocks, add_rows, jnp.zeros((LISTS, D), jnp.float32))
    diag_term = perp_weight * member_counts.astype(jnp.float32)[:, None] + prior_weight
    centroids = old_centroids
    residual = aniso_par * row_sums + prior_weight * centroids - (diag_term * centroids + (aniso_par - perp_weight) * gram_all(centroids))
    direction = residual
    norm_now = lax.optimization_barrier(jnp.sum(residual * residual, axis=1, keepdims=True))
    for iteration in range(ITERS):
        applied = diag_term * direction + (aniso_par - perp_weight) * gram_all(direction)
        step_len = norm_now / lax.optimization_barrier(jnp.sum(direction * applied, axis=1, keepdims=True))
        centroids = centroids + step_len * direction
        residual = residual - step_len * applied
        norm_next = lax.optimization_barrier(jnp.sum(residual * residual, axis=1, keepdims=True))
        direction = residual + norm_next / norm_now * direction
        norm_now = norm_next
    panel = centroids.astype(jnp.bfloat16)
    blocks = next_rows.reshape(NEXT // NEXT_DEV, NEXT_DEV, D)

    def score_block(piece_block):
        return lax.optimization_barrier(jnp.max(jnp.dot(piece_block, panel.T, preferred_element_type=jnp.float32), axis=1))
    top_score = lax.map(score_block, blocks).reshape(NEXT)
    return (centroids, top_score / D)
```

```python
import jax
import jax.numpy as jnp
from jax import lax
from jax.experimental import pallas as pl
from jax.experimental.pallas import tpu as pltpu
from jax.sharding import PartitionSpec as P

MESH = pl.DeviceIdType.MESH
F32 = jnp.float32
BF16 = jnp.bfloat16
I32 = jnp.int32

ITERS = 3
N_LIST = 64
N_ROW = 4
LO = 64
D = 768
H = D // 2
ROWS_DEV = 1024
NEXT_DEV = 1536
CAP = 24
CAP2 = 2 * CAP
GROUP = 16
QUARTER = LO // N_ROW
SHARDS = 32

eps_norm = 1e-06
aniso_par = 32.0
perp_weight = 1.0
prior_weight = 16.0
gram_weight = aniso_par - perp_weight


def nt(a, b):
    return lax.dot_general(a, b, (((1,), (1,)), ((), ())), preferred_element_type=F32)


def nn(a, b):
    return lax.dot_general(a, b, (((1,), (0,)), ((), ())), preferred_element_type=F32)


def split_pair(values):
    high_part = values.astype(BF16)
    low_part = (values - high_part.astype(F32)).astype(BF16)
    return high_part, low_part


def iota(shape, dim):
    return lax.broadcasted_iota(I32, shape, dim)


def wait_for(ref, sem):
    pltpu.make_async_copy(ref, ref, sem).wait()


def kernel(
    corpus, row_list, list_slot, counts, old, next_hbm,
    out_cent, out_best,
    key, ids_send, send, ids_recv, recv, unit, member,
    first, first_in, gram_all, direction, grams, grams_in, dots, dots_in,
    diag, pan, next_all, best, best_in,
    a2a_send, a2a_recv, ids_send_sem, ids_recv_sem,
    next_sem, first_sem, dir_sem, gram_sem, dot_sem, cent_sem,
    z_sem, one_sem, two_sem, two_recv, best_sem,
):
    l = lax.axis_index("list")
    r = lax.axis_index("row")
    c = l % 2
    x = (l // 2) % 4
    y = (l // 8) % 4
    zl = l // 32

    def list_of(zl_, y_, x_, c_):
        return ((zl_ * 4 + y_) * 4 + x_) * 2 + c_

    mine = (y - x + 4) % 4
    place = mine * GROUP + zl * 8 + x * 2 + c

    def list_at(group, member_):
        zl_ = member_ // 8
        x_ = (member_ // 2) % 4
        return list_of(zl_, (x_ + group) % 4, x_, member_ % 2)

    barrier = pltpu.get_barrier_semaphore()

    def greet(k, carry):
        pl.semaphore_signal(
            barrier, inc=1, device_id={"list": (l + k) % N_LIST, "row": r}, device_id_type=MESH
        )
        return carry

    lax.fori_loop(1, N_LIST, greet, 0)
    for k in range(1, N_ROW):
        for z_ in range(2):
            pl.semaphore_signal(
                barrier,
                inc=1,
                device_id={"list": list_of((zl + z_) % 2, y, x, c), "row": (r + k) % N_ROW},
                device_id_type=MESH,
            )

    own_next = pltpu.make_async_copy(next_hbm, next_all.at[c], next_sem.at[0])
    own_next.start()

    ids_row = row_list[...]
    table = list_slot[...]
    table2 = jnp.concatenate([(table // LO) * LO, table % LO], axis=0).astype(F32)
    high = ids_row // 128
    low = ids_row % 128
    pick = (iota((32, ROWS_DEV), 0) == high).astype(F32)
    pick2 = jnp.concatenate([pick, pick], axis=0).astype(BF16)
    looked = nn(table2.T.astype(BF16), pick2)
    slot = jnp.sum(
        jnp.where(iota((128, ROWS_DEV), 0) == low, looked, 0.0), axis=0, keepdims=True
    ).astype(I32)
    owner = slot // LO
    local = slot % LO
    oc = owner % 2
    ox = (owner // 2) % 4
    oy = (owner // 8) % 4
    oz = owner // 32
    spot = ((oy - ox + 4) % 4) * GROUP + oz * 8 + ox * 2 + oc
    hit = iota((N_LIST, ROWS_DEV), 0) == spot
    hits = hit.astype(F32)
    before = (iota((256, 256), 0) < iota((256, 256), 1)).astype(F32).astype(BF16)
    carry = jnp.zeros((N_LIST, 1), F32)
    ranks = []
    for b in range(ROWS_DEV // 256):
        part = hits[:, b * 256 : (b + 1) * 256]
        ranks.append(nn(part.astype(BF16), before) + carry)
        carry = carry + jnp.sum(part, axis=1, keepdims=True)
    rank = jnp.concatenate(ranks, axis=1)
    key[...] = jnp.where(hit, rank, -1.0).astype(I32)
    rank_row = jnp.sum(hits * rank, axis=0, keepdims=True).astype(I32)
    named = (hits * (local + 1).astype(F32)).astype(BF16)
    at_rank = (iota((128, ROWS_DEV), 0) == rank_row).astype(F32).astype(BF16)
    ids_send[...] = nt(named, at_rank) - 1.0

    pl.semaphore_wait(barrier, N_LIST - 1 + 2 * (N_ROW - 1))

    def send_group(chunk, carry_):
        group = (mine + chunk) % 4
        keys = key[pl.ds(pl.multiple_of(group * GROUP, GROUP), GROUP), :]
        chosen = keys.reshape(GROUP, 1, ROWS_DEV) == iota((GROUP, CAP, ROWS_DEV), 1)
        chosen = chosen.astype(F32).reshape(GROUP * CAP, ROWS_DEV).astype(BF16)
        rows = nn(chosen, corpus[...]).reshape(GROUP, CAP, D)
        rows = jnp.concatenate([rows[:, :, :H], rows[:, :, H:]], axis=1)
        send[pl.ds(pl.multiple_of(group * GROUP * CAP2, GROUP * CAP2), GROUP * CAP2), :] = (
            rows.reshape(GROUP * CAP2, H).astype(BF16)
        )

        def send_one(j, carry2):
            m = (place % GROUP + j) % GROUP
            to = group * GROUP + m

            @pl.when(to != place)
            def _():
                device = {"list": list_at(group, m), "row": r}
                pltpu.make_async_remote_copy(
                    src_ref=ids_send.at[pl.ds(to, 1)],
                    dst_ref=ids_recv.at[pl.ds(place, 1)],
                    send_sem=ids_send_sem,
                    recv_sem=ids_recv_sem.at[chunk],
                    device_id=device,
                    device_id_type=MESH,
                ).start()
                pltpu.make_async_remote_copy(
                    src_ref=send.at[pl.ds(pl.multiple_of(to * CAP2, CAP2), CAP2)],
                    dst_ref=recv.at[pl.ds(pl.multiple_of(place * CAP2, CAP2), CAP2)],
                    send_sem=a2a_send,
                    recv_sem=a2a_recv.at[chunk],
                    device_id=device,
                    device_id_type=MESH,
                ).start()

            return carry2

        lax.fori_loop(0, GROUP, send_one, 0)
        return carry_

    lax.fori_loop(0, 4, send_group, 0)
    own_block = pl.ds(pl.multiple_of(place * CAP2, CAP2), CAP2)
    recv[own_block, :] = send[own_block, :]
    ids_recv[pl.ds(place, 1), :] = ids_send[pl.ds(place, 1), :]

    other_core = {"list": list_of(zl, y, x, 1 - c), "row": r}
    swap = pltpu.make_async_remote_copy(
        src_ref=next_hbm,
        dst_ref=next_all.at[c],
        send_sem=next_sem.at[1],
        recv_sem=next_sem.at[2],
        device_id=other_core,
        device_id_type=MESH,
    )
    swap.start()

    count_row = counts[...].astype(F32)
    square = iota((LO, LO), 0) == iota((LO, LO), 1)
    count_col = jnp.sum(jnp.where(square, count_row, 0.0), axis=1, keepdims=True)
    diag[...] = jnp.broadcast_to(perp_weight * count_col + prior_weight, (LO, 128))

    old_high, old_low = split_pair(old[...])
    old_two = jnp.concatenate([old_high, old_low], axis=0)
    width = GROUP * CAP
    source_of = (iota((GROUP, width), 1) * 2731) // 65536
    lane = iota((128, width), 1)
    spread = (lane - ((lane * 2731) // 65536) * CAP == iota((128, width), 0)).astype(F32).astype(BF16)
    first[...] = jnp.zeros_like(first)

    def take_group(chunk, carry_):
        group = (mine - chunk + 4) % 4

        @pl.when(chunk == 0)
        def _():
            wait_for(ids_recv.at[pl.ds(0, GROUP - 1)], ids_recv_sem.at[0])
            wait_for(recv.at[pl.ds(0, (GROUP - 1) * CAP2)], a2a_recv.at[0])

        @pl.when(chunk > 0)
        def _():
            wait_for(ids_recv.at[pl.ds(0, GROUP)], ids_recv_sem.at[chunk])
            wait_for(recv.at[pl.ds(0, GROUP * CAP2)], a2a_recv.at[chunk])

        named_in = ids_recv[pl.ds(pl.multiple_of(group * GROUP, GROUP), GROUP), :]
        wide = nn(named_in.astype(BF16), spread)
        flat = jnp.sum(
            jnp.where(source_of == iota((GROUP, width), 0), wide, 0.0), axis=0, keepdims=True
        ).astype(I32)
        own = (iota((LO, width), 0) == flat).astype(F32)
        member[:, pl.ds(pl.multiple_of(group * width, width), width)] = own
        raw = recv[pl.ds(pl.multiple_of(group * GROUP * CAP2, GROUP * CAP2), GROUP * CAP2), :]
        raw = raw.astype(F32).reshape(GROUP, CAP2, H)
        rows = jnp.concatenate(
            [raw[:, :CAP, :].reshape(width, H), raw[:, CAP:, :].reshape(width, H)], axis=1
        )
        inverse = lax.rsqrt(jnp.sum(rows * rows, axis=1, keepdims=True) + eps_norm)
        units = (rows * inverse).astype(BF16)
        unit[pl.ds(pl.multiple_of(group * width, width), width), :] = units
        scores = nt(old_two, units)
        scores = (scores[:LO] + scores[LO:]) * own * (-gram_weight)
        wgt_high, wgt_low = split_pair(scores)
        first[...] += (
            nn((own * aniso_par).astype(BF16), rows.astype(BF16))
            + nn(wgt_high, units)
            + nn(wgt_low, units)
        )
        return carry_

    lax.fori_loop(0, 4, take_group, 0)

    quarter = pl.ds(pl.multiple_of(r * QUARTER, QUARTER), QUARTER)

    def peer(k):
        return (r + k) % N_ROW

    def rows_of(k):
        return pl.ds(pl.multiple_of(peer(k) * QUARTER, QUARTER), QUARTER)

    def scatter(source, target, send_sem, recv_sem):
        for k in (1, 3, 2):
            pltpu.make_async_remote_copy(
                src_ref=source.at[rows_of(k)],
                dst_ref=target.at[quarter],
                send_sem=send_sem,
                recv_sem=recv_sem,
                device_id={"list": l, "row": peer(k)},
                device_id_type=MESH,
            ).start()

    def gather(ref, send_sem, recv_sem):
        for k in (1, 3, 2):
            pltpu.make_async_remote_copy(
                src_ref=ref.at[quarter],
                dst_ref=ref.at[quarter],
                send_sem=send_sem,
                recv_sem=recv_sem,
                device_id={"list": l, "row": peer(k)},
                device_id_type=MESH,
            ).start()

    three = pl.ds(0, 3 * QUARTER)
    scatter(first, first_in, first_sem.at[0], first_sem.at[1])
    wait_for(first_in.at[three], first_sem.at[1])
    old_own = old[quarter, :]
    diag_own = diag[quarter, :][:, :1]
    residual = first[quarter, :] + (prior_weight - diag_own) * old_own
    for k in range(1, N_ROW):
        residual = residual + first_in[rows_of(k), :]
    centroid = old_own
    moved = residual
    norm_now = jnp.sum(residual * residual, axis=1, keepdims=True)
    for step in range(ITERS):
        dir_now = direction.at[step]
        dir_now[quarter, :] = moved.astype(BF16)
        moved = moved.astype(BF16).astype(F32)
        gather(dir_now, dir_sem.at[2 * step], dir_sem.at[2 * step + 1])
        wait_for(dir_now.at[three], dir_sem.at[2 * step + 1])
        scores = nt(dir_now[...], unit[...]) * member[...]
        if step < ITERS - 1:
            gram = nn(scores.astype(BF16), unit[...])
            grams[step] = gram.astype(BF16)
            gram_all[...] = gram
            scatter(
                grams.at[step], grams_in.at[step], gram_sem.at[2 * step], gram_sem.at[2 * step + 1]
            )
            wait_for(grams_in.at[step].at[three], gram_sem.at[2 * step + 1])
            total = gram_all[quarter, :]
            for k in range(1, N_ROW):
                total = total + grams_in.at[step][rows_of(k), :].astype(F32)
            applied = diag_own * moved + gram_weight * total
            step_len = norm_now / jnp.sum(moved * applied, axis=1, keepdims=True)
            centroid = centroid + step_len * moved
            residual = residual - step_len * applied
            norm_next = jnp.sum(residual * residual, axis=1, keepdims=True)
            moved = residual + norm_next / norm_now * moved
            norm_now = norm_next
        else:
            squares = jnp.sum(scores * scores, axis=1, keepdims=True)
            dots[...] = jnp.broadcast_to(squares, (LO, 128))
            scatter(dots, dots_in, dot_sem.at[0], dot_sem.at[1])
            wait_for(dots_in.at[three], dot_sem.at[1])
            total = dots[quarter, :]
            for k in range(1, N_ROW):
                total = total + dots_in[rows_of(k), :]
            bend = diag_own * jnp.sum(moved * moved, axis=1, keepdims=True)
            step_len = norm_now / (bend + gram_weight * total[:, :1])
            centroid = centroid + step_len * moved

    a_own = (y * 4 + x) * LO
    b_own = (16 + x * 4 + y) * LO
    pan_own = (1 - zl) * a_own + zl * b_own
    piece = pl.ds(pl.multiple_of(pan_own + r * QUARTER, QUARTER), QUARTER)
    pan[piece, :] = centroid.astype(BF16)
    for k in range(N_ROW):
        for z_ in range(2):
            if k == 0 and z_ == 0:
                continue
            pltpu.make_async_remote_copy(
                src_ref=pan.at[piece],
                dst_ref=pan.at[piece],
                send_sem=z_sem.at[0],
                recv_sem=z_sem.at[1],
                device_id={"list": list_of((zl + z_) % 2, y, x, c), "row": peer(k)},
                device_id_type=MESH,
            ).start()
    out_cent[quarter, :] = centroid
    wait_for(pan.at[pl.ds(0, 7 * QUARTER)], z_sem.at[1])

    def at(start, n):
        return pl.ds(pl.multiple_of(start, LO), n)

    for k in (1, 3, 2):
        for half, start, device in (
            (0, a_own, list_of(zl, y, (x + k) % 4, c)),
            (1, b_own, list_of(zl, (y + k) % 4, x, c)),
        ):
            pltpu.make_async_remote_copy(
                src_ref=pan.at[at(start, LO)],
                dst_ref=pan.at[at(start, LO)],
                send_sem=one_sem.at[half],
                recv_sem=one_sem.at[2 + half],
                device_id={"list": device, "row": r},
                device_id_type=MESH,
            ).start()
    own_next.wait()
    swap.wait_recv()
    for half in range(2):
        wait_for(pan.at[pl.ds(0, 3 * LO)], one_sem.at[2 + half])
    a_four = y * 4 * LO
    b_four = (16 + x * 4) * LO
    for k in (1, 3, 2):
        for half, start, device in (
            (0, a_four, list_of(zl, (y + k) % 4, x, c)),
            (1, b_four, list_of(zl, y, (x + k) % 4, c)),
        ):
            pltpu.make_async_remote_copy(
                src_ref=pan.at[at(start, 4 * LO)],
                dst_ref=pan.at[at(start, 4 * LO)],
                send_sem=two_sem.at[half],
                recv_sem=two_recv.at[half * 4 + k],
                device_id={"list": device, "row": r},
                device_id_type=MESH,
            ).start()
    gather(out_cent, cent_sem.at[0], cent_sem.at[1])

    best[...] = jnp.full_like(best, -jnp.inf)

    def score_chunk(step, carry_):
        half = step % 2
        order = step // 2
        dist = order + (order == 2).astype(I32) - (order == 3).astype(I32)
        spot_ = (1 - half) * y + half * x
        start = half * 16 * LO + ((spot_ - dist + 4) % 4) * 4 * LO

        @pl.when(order > 0)
        def _():
            wait_for(pan.at[pl.ds(0, 4 * LO)], two_recv.at[half * 4 + dist])

        block = pan[pl.ds(pl.multiple_of(start, 4 * LO), 4 * LO), :]

        for core in range(2):
            for b in range(NEXT_DEV // 512):
                found = nt(block, next_all[core, b * 512 : (b + 1) * 512, :])
                top = jnp.max(found.reshape(4 * LO // 8, 8, 512), axis=0)
                lanes = slice(b * 512, (b + 1) * 512)
                best[core, :, lanes] = jnp.maximum(best[core, :, lanes], top)
        return carry_

    lax.fori_loop(0, 8, score_chunk, 0)

    top_other = jnp.max(best[1 - c], axis=0, keepdims=True)
    best_in[0] = top_other
    back = pltpu.make_async_remote_copy(
        src_ref=best_in.at[0],
        dst_ref=best_in.at[1],
        send_sem=best_sem.at[0],
        recv_sem=best_sem.at[1],
        device_id=other_core,
        device_id_type=MESH,
    )
    back.start()
    top_own = jnp.max(best[c], axis=0, keepdims=True)
    wait_for(out_cent.at[three], cent_sem.at[1])

    wait_for(ids_send.at[pl.ds(0, N_LIST - 1)], ids_send_sem)
    wait_for(send.at[pl.ds(0, (N_LIST - 1) * CAP2)], a2a_send)
    swap.wait_send()
    wait_for(first.at[three], first_sem.at[0])
    for step in range(ITERS):
        wait_for(direction.at[step].at[three], dir_sem.at[2 * step])
    for step in range(ITERS - 1):
        wait_for(grams.at[step].at[three], gram_sem.at[2 * step])
    wait_for(dots.at[three], dot_sem.at[0])
    wait_for(pan.at[pl.ds(0, 7 * QUARTER)], z_sem.at[0])
    for half in range(2):
        wait_for(pan.at[pl.ds(0, 3 * LO)], one_sem.at[half])
        wait_for(pan.at[pl.ds(0, 12 * LO)], two_sem.at[half])
    wait_for(out_cent.at[three], cent_sem.at[0])
    back.wait()
    out_best[...] = jnp.maximum(top_own, best_in[1]) / D


def on_device(corpus, row_list, list_slot, member_counts, old_centroids, next_rows):
    vmem = pl.BlockSpec(memory_space=pltpu.VMEM)
    dma = pltpu.SemaphoreType.DMA
    cent, best = pl.pallas_call(
        kernel,
        out_shape=(
            jax.ShapeDtypeStruct((LO, D), F32),
            jax.ShapeDtypeStruct((1, NEXT_DEV), F32),
        ),
        in_specs=[vmem] * 5 + [pl.BlockSpec(memory_space=pl.ANY)],
        out_specs=(vmem, vmem),
        scratch_shapes=[
            pltpu.VMEM((N_LIST, ROWS_DEV), I32),
            pltpu.VMEM((N_LIST, 128), F32),
            pltpu.VMEM((N_LIST * CAP2, H), BF16),
            pltpu.VMEM((N_LIST, 128), F32),
            pltpu.VMEM((N_LIST * CAP2, H), BF16),
            pltpu.VMEM((N_LIST * CAP, D), BF16),
            pltpu.VMEM((LO, N_LIST * CAP), F32),
            pltpu.VMEM((LO, D), F32),
            pltpu.VMEM((LO, D), F32),
            pltpu.VMEM((LO, D), F32),
            pltpu.VMEM((ITERS, LO, D), BF16),
            pltpu.VMEM((ITERS - 1, LO, D), BF16),
            pltpu.VMEM((ITERS - 1, LO, D), BF16),
            pltpu.VMEM((LO, 128), F32),
            pltpu.VMEM((LO, 128), F32),
            pltpu.VMEM((LO, 128), F32),
            pltpu.VMEM((SHARDS * LO, D), BF16),
            pltpu.VMEM((2, NEXT_DEV, D), BF16),
            pltpu.VMEM((2, 8, NEXT_DEV), F32),
            pltpu.VMEM((2, 1, NEXT_DEV), F32),
            dma, dma((4,)), dma, dma((4,)),
            dma((3,)), dma((2,)), dma((2 * ITERS,)), dma((2 * ITERS - 2,)), dma((2,)), dma((2,)),
            dma((2,)), dma((4,)), dma((2,)), dma((8,)), dma((2,)),
        ],
        compiler_params=pltpu.CompilerParams(
            collective_id=0, has_side_effects=True, vmem_limit_bytes=56 * 2**20
        ),
    )(
        corpus,
        row_list.reshape(1, ROWS_DEV),
        list_slot.reshape(32, 128),
        member_counts.reshape(1, LO),
        old_centroids,
        next_rows,
    )
    return cent, best.reshape(NEXT_DEV)


def solution(mesh):
    in_specs = (
        P(("list", "row"), None),
        P(("list", "row")),
        P(),
        P("list"),
        P("list", None),
        P(("list", "row"), None),
    )
    out_specs = (P("list", None), P(("list", "row")))
    return jax.shard_map(
        on_device, mesh=mesh, in_specs=in_specs, out_specs=out_specs, check_vma=False
    )
```

```python
import itertools

import jax
import jax.numpy as jnp
from jax import lax
from jax.experimental import pallas as pl
from jax.experimental.pallas import tpu as pltpu
from jax.sharding import PartitionSpec as P

MESH = pl.DeviceIdType.MESH
F32 = jnp.float32
BF16 = jnp.bfloat16
I32 = jnp.int32

ITERS = 3
N_LIST = 64
N_ROW = 4
LO = 64
D = 768
H = D // 2
ROWS_DEV = 1024
NEXT_DEV = 1536
CAP = 24
CAP2 = 2 * CAP
GROUP = 16
QUARTER = LO // N_ROW
SHARDS = 16
HALF = NEXT_DEV // 2
PIECE = HALF // 2
AWAY = 6 * HALF
RING = (0, 1, 2, 1)
SEND_ORDER = (1, 3, 2, 0)
NEAR = AWAY + NEXT_DEV

eps_norm = 1e-06
aniso_par = 32.0
perp_weight = 1.0
prior_weight = 16.0
gram_weight = aniso_par - perp_weight


def nt(a, b):
    return lax.dot_general(a, b, (((1,), (1,)), ((), ())), preferred_element_type=F32)


def nn(a, b):
    return lax.dot_general(a, b, (((1,), (0,)), ((), ())), preferred_element_type=F32)


def split_pair(values):
    high_part = values.astype(BF16)
    low_part = (values - high_part.astype(F32)).astype(BF16)
    return high_part, low_part


def iota(shape, dim):
    return lax.broadcasted_iota(I32, shape, dim)


def wait_for(ref, sem):
    pltpu.make_async_copy(ref, ref, sem).wait()


def kernel(
    corpus_hbm, row_list, list_slot, counts, old, next_hbm,
    out_cent, out_best,
    corpus, key, ids_send, send, ids_recv, recv, unit, member,
    first, first_high, first_low, high_in, low_in, gram_all, direction, grams, grams_in,
    last, dots_in, diag, pan, nexts, best, best_in,
    corpus_sem, a2a_send, a2a_recv, ids_send_sem, ids_recv_sem,
    high_sem, low_sem, dir_sem, gram_sem, last_sem, dot_sem,
    next_sem, next_send, next_recv, pan_send, pan_recv, core_send, core_recv, best_sem,
):
    l = lax.axis_index("list")
    r = lax.axis_index("row")
    c = l % 2
    x = (l // 2) % 4
    y = (l // 8) % 4
    zl = l // 32

    def list_of(zl_, y_, x_, c_):
        return ((zl_ * 4 + y_) * 4 + x_) * 2 + c_

    mine = (y - x + 4) % 4
    place = mine * GROUP + zl * 8 + x * 2 + c

    z_part = [zl * 32, (1 - zl) * 32]
    y_part = [((y + k) % 4) * 8 for k in range(4)]
    x_at = [(x + k) % 4 for k in range(4)]
    c_at = [c, 1 - c]

    beyond = (r + 2 * zl - 1 + N_ROW) % N_ROW
    row_core = [r + (beyond - r) * c_at[k] for k in range(2)]
    row_from = [[r, r], row_core]
    row_to = [r, row_core[0]]

    def chip(dx, dy, dz=0):
        spot_ = list_of(zl if dz == 0 else 1 - zl, (y + dy + 4) % 4, (x + dx + 4) % 4, c)
        row = r if dz == 0 else (r + zl + (0 if dz > 0 else N_ROW - 1)) % N_ROW
        return {"list": spot_, "row": row}

    twos = ((0, 0), (2, 0), (0, 2), (2, 2))

    barrier = pltpu.get_barrier_semaphore()

    def greet_device(device):
        pl.semaphore_signal(barrier, inc=1, device_id=device, device_id_type=MESH)

    for k in (2, 1, 3):
        greet_device({"list": l, "row": (r + k) % N_ROW})
    for dx, dy in twos[::-1]:
        for dz in (1, -1):
            greet_device(chip(dx, dy, dz))
    offsets = itertools.product(range(4), range(4), range(2), range(2))
    for dy, dx, dz, dc in sorted(offsets, key=lambda o: -RING[o[0]] - RING[o[1]] - o[2]):
        if dy or dx or dz or dc:
            other = z_part[dz] + y_part[dy] + x_at[dx] * 2 + c_at[dc]
            greet_device({"list": other, "row": row_from[dz][dc]})

    own_corpus = pltpu.make_async_copy(corpus_hbm, corpus, corpus_sem)
    own_corpus.start()
    own_next = pltpu.make_async_copy(next_hbm, nexts.at[pl.ds(AWAY, NEXT_DEV)], next_sem)
    own_next.start()

    ids_row = row_list[...]
    table = list_slot[...]
    table2 = jnp.concatenate([(table // LO) * LO, table % LO], axis=0).astype(F32)
    high = ids_row // 128
    low = ids_row % 128
    pick = (iota((32, ROWS_DEV), 0) == high).astype(F32)
    pick2 = jnp.concatenate([pick, pick], axis=0).astype(BF16)
    looked = nn(table2.T.astype(BF16), pick2)
    slot = jnp.sum(
        jnp.where(iota((128, ROWS_DEV), 0) == low, looked, 0.0), axis=0, keepdims=True
    ).astype(I32)
    owner = slot // LO
    local = slot % LO
    oc = owner % 2
    ox = (owner // 2) % 4
    oy = (owner // 8) % 4
    oz = owner // 32
    spot = ((oy - ox + 4) % 4) * GROUP + oz * 8 + ox * 2 + oc
    hit = iota((N_LIST, ROWS_DEV), 0) == spot
    hits = hit.astype(F32)
    before = (iota((256, 256), 0) < iota((256, 256), 1)).astype(F32).astype(BF16)
    carry = jnp.zeros((N_LIST, 1), F32)
    ranks = []
    for b in range(ROWS_DEV // 256):
        part = hits[:, b * 256 : (b + 1) * 256]
        ranks.append(nn(part.astype(BF16), before) + carry)
        carry = carry + jnp.sum(part, axis=1, keepdims=True)
    rank = jnp.concatenate(ranks, axis=1)
    key[...] = jnp.where(hit, rank, -1.0).astype(I32)
    rank_row = jnp.sum(hits * rank, axis=0, keepdims=True).astype(I32)
    named = (hits * (local + 1).astype(F32)).astype(BF16)
    at_rank = (iota((128, ROWS_DEV), 0) == rank_row).astype(F32).astype(BF16)
    ids_send[...] = nt(named, at_rank) - 1.0

    own_corpus.wait()
    pl.semaphore_wait(barrier, N_LIST - 1 + N_ROW - 1 + 8)

    def send_group(chunk, carry_):
        group = (mine + chunk) % 4
        keys = key[pl.ds(pl.multiple_of(group * GROUP, GROUP), GROUP), :]
        chosen = keys.reshape(GROUP, 1, ROWS_DEV) == iota((GROUP, CAP, ROWS_DEV), 1)
        chosen = chosen.astype(F32).reshape(GROUP * CAP, ROWS_DEV).astype(BF16)
        rows = nn(chosen, corpus[...]).reshape(GROUP, CAP, D)
        rows = jnp.concatenate([rows[:, :, :H], rows[:, :, H:]], axis=1)
        send[pl.ds(pl.multiple_of(group * GROUP * CAP2, GROUP * CAP2), GROUP * CAP2), :] = (
            rows.reshape(GROUP * CAP2, H).astype(BF16)
        )

        def send_one(to, device):
            pltpu.make_async_remote_copy(
                src_ref=ids_send.at[pl.ds(to, 1)],
                dst_ref=ids_recv.at[pl.ds(place, 1)],
                send_sem=ids_send_sem,
                recv_sem=ids_recv_sem.at[chunk],
                device_id=device,
                device_id_type=MESH,
            ).start()
            pltpu.make_async_remote_copy(
                src_ref=send.at[pl.ds(pl.multiple_of(to * CAP2, CAP2), CAP2)],
                dst_ref=recv.at[pl.ds(pl.multiple_of(place * CAP2, CAP2), CAP2)],
                send_sem=a2a_send,
                recv_sem=a2a_recv.at[chunk],
                device_id=device,
                device_id_type=MESH,
            ).start()

        for dx in SEND_ORDER:
            y_part_ = ((y + dx + chunk) % 4) * 8
            for dz in (1, 0):
                for dc in range(2):
                    to = group * GROUP + z_part[dz] // 4 + x_at[dx] * 2 + c_at[dc]
                    device = {
                        "list": z_part[dz] + y_part_ + x_at[dx] * 2 + c_at[dc],
                        "row": row_to[dz],
                    }
                    if dx or dz or dc:
                        send_one(to, device)
                    else:
                        pl.when(chunk > 0)(lambda to=to, device=device: send_one(to, device))

        return carry_

    lax.fori_loop(0, 4, send_group, 0)
    own_block = pl.ds(pl.multiple_of(place * CAP2, CAP2), CAP2)
    recv[own_block, :] = send[own_block, :]
    ids_recv[pl.ds(place, 1), :] = ids_send[pl.ds(place, 1), :]

    count_row = counts[...].astype(F32)
    square = iota((LO, LO), 0) == iota((LO, LO), 1)
    count_col = jnp.sum(jnp.where(square, count_row, 0.0), axis=1, keepdims=True)
    diag[...] = jnp.broadcast_to(perp_weight * count_col + prior_weight, (LO, 128))

    def pass_on(start, to_set, part, device, at):
        pltpu.make_async_remote_copy(
            src_ref=nexts.at[pl.ds(start, PIECE)],
            dst_ref=nexts.at[pl.ds(to_set * HALF + part * PIECE, PIECE)],
            send_sem=next_send,
            recv_sem=next_recv.at[at],
            device_id=device,
            device_id_type=MESH,
        ).start()

    sides = ((1, 0), (-1, 0), (0, 1), (0, -1))

    old_high, old_low = split_pair(old[...])
    old_two = jnp.concatenate([old_high, old_low], axis=0)
    width = GROUP * CAP
    source_of = (iota((GROUP, width), 1) * 2731) // 65536
    lane = iota((128, width), 1)
    spread = (lane - ((lane * 2731) // 65536) * CAP == iota((128, width), 0)).astype(F32).astype(BF16)
    first[...] = jnp.zeros_like(first)

    def take_group(chunk, carry_):
        group = (mine - chunk + 4) % 4

        @pl.when(chunk == 0)
        def _():
            wait_for(ids_recv.at[pl.ds(0, GROUP - 1)], ids_recv_sem.at[0])
            wait_for(recv.at[pl.ds(0, (GROUP - 1) * CAP2)], a2a_recv.at[0])

        @pl.when(chunk > 0)
        def _():
            wait_for(ids_recv.at[pl.ds(0, GROUP)], ids_recv_sem.at[chunk])
            wait_for(recv.at[pl.ds(0, GROUP * CAP2)], a2a_recv.at[chunk])

        @pl.when(chunk == 3)
        def _():
            own_next.wait()
            for j, (dx, dy) in enumerate(sides):
                pass_on(AWAY + (j % 2) * HALF + (j // 2) * PIECE, j, j // 2, chip(dx, dy), j)

        named_in = ids_recv[pl.ds(pl.multiple_of(group * GROUP, GROUP), GROUP), :]
        wide = nn(named_in.astype(BF16), spread)
        flat = jnp.sum(
            jnp.where(source_of == iota((GROUP, width), 0), wide, 0.0), axis=0, keepdims=True
        ).astype(I32)
        own = (iota((LO, width), 0) == flat).astype(F32)
        member[:, pl.ds(pl.multiple_of(group * width, width), width)] = own
        raw = recv[pl.ds(pl.multiple_of(group * GROUP * CAP2, GROUP * CAP2), GROUP * CAP2), :]
        raw = raw.astype(F32).reshape(GROUP, CAP2, H)
        rows = jnp.concatenate(
            [raw[:, :CAP, :].reshape(width, H), raw[:, CAP:, :].reshape(width, H)], axis=1
        )
        inverse = lax.rsqrt(jnp.sum(rows * rows, axis=1, keepdims=True) + eps_norm)
        units = (rows * inverse).astype(BF16)
        unit[pl.ds(pl.multiple_of(group * width, width), width), :] = units
        scores = nt(old_two, units)
        scores = (scores[:LO] + scores[LO:]) * own * (-gram_weight)
        wgt_high, wgt_low = split_pair(scores)
        first[...] += (
            nn((own * aniso_par).astype(BF16), rows.astype(BF16))
            + nn(wgt_high, units)
            + nn(wgt_low, units)
        )
        return carry_

    lax.fori_loop(0, 4, take_group, 0)

    quarter = pl.ds(pl.multiple_of(r * QUARTER, QUARTER), QUARTER)

    def peer(k):
        return (r + k) % N_ROW

    def rows_of(k):
        return pl.ds(pl.multiple_of(peer(k) * QUARTER, QUARTER), QUARTER)

    def scatter(source, target, send_sem, recv_sem):
        for k in (1, 3, 2):
            pltpu.make_async_remote_copy(
                src_ref=source.at[rows_of(k)],
                dst_ref=target.at[quarter],
                send_sem=send_sem,
                recv_sem=recv_sem,
                device_id={"list": l, "row": peer(k)},
                device_id_type=MESH,
            ).start()

    def gather(ref, send_sem, recv_sem):
        for k in (1, 3, 2):
            pltpu.make_async_remote_copy(
                src_ref=ref.at[quarter],
                dst_ref=ref.at[quarter],
                send_sem=send_sem,
                recv_sem=recv_sem,
                device_id={"list": l, "row": peer(k)},
                device_id_type=MESH,
            ).start()

    three = pl.ds(0, 3 * QUARTER)

    def pass_more():
        for j in range(4):
            wait_for(nexts.at[pl.ds(0, PIECE)], next_recv.at[j])
        for j, (dx, dy) in enumerate(sides):
            part = j // 2
            over = chip(dy, dx)
            pass_on(j * HALF + part * PIECE, 4 + j % 2, part, over, 8 + j)
            pass_on(AWAY + (j % 2) * HALF + (1 - part) * PIECE, j, 1 - part, chip(dx, dy), 4 + j)

    high_part, low_part = split_pair(first[...])
    first_high[...] = high_part
    first_low[...] = low_part
    scatter(first_high, high_in, high_sem.at[0], high_sem.at[1])
    scatter(first_low, low_in, low_sem.at[0], low_sem.at[1])
    old_own = old[quarter, :]
    diag_own = diag[quarter, :][:, :1]
    residual = first[quarter, :] + (prior_weight - diag_own) * old_own
    wait_for(high_in.at[three], high_sem.at[1])
    for k in range(1, N_ROW):
        residual = residual + high_in[rows_of(k), :].astype(F32)
    centroid = old_own
    moved = residual
    for step in range(ITERS):
        dir_now = direction.at[step]
        dir_now[quarter, :] = moved.astype(BF16)
        moved = moved.astype(BF16).astype(F32)
        gather(dir_now, dir_sem.at[2 * step], dir_sem.at[2 * step + 1])
        if step == ITERS - 1:
            last[quarter, :D] = centroid
            last[quarter, D:] = jnp.broadcast_to(norm_now, (QUARTER, 128))
            gather(last, last_sem.at[0], last_sem.at[1])
        wait_for(dir_now.at[three], dir_sem.at[2 * step + 1])
        scores = nt(dir_now[...], unit[...]) * member[...]
        if step == ITERS - 1:
            break
        gram = nn(scores.astype(BF16), unit[...])
        grams[step] = gram.astype(BF16)
        gram_all[...] = gram
        scatter(
            grams.at[step], grams_in.at[step], gram_sem.at[2 * step], gram_sem.at[2 * step + 1]
        )
        if step == 0:
            pass_more()
            wait_for(low_in.at[three], low_sem.at[1])
            for k in range(1, N_ROW):
                residual = residual + low_in[rows_of(k), :].astype(F32)
            norm_now = jnp.sum(residual * residual, axis=1, keepdims=True)
        wait_for(grams_in.at[step].at[three], gram_sem.at[2 * step + 1])
        total = gram_all[quarter, :]
        for k in range(1, N_ROW):
            total = total + grams_in.at[step][rows_of(k), :].astype(F32)
        applied = diag_own * moved + gram_weight * total
        step_len = norm_now / jnp.sum(moved * applied, axis=1, keepdims=True)
        centroid = centroid + step_len * moved
        residual = residual - step_len * applied
        norm_next = jnp.sum(residual * residual, axis=1, keepdims=True)
        moved = residual + norm_next / norm_now * moved
        norm_now = norm_next

    squares = jnp.sum(scores * scores, axis=1, keepdims=True)
    squares = jnp.sum(jnp.where(square, squares, 0.0), axis=0, keepdims=True)
    dots_in[pl.ds(r, 1), :] = jnp.concatenate([squares, squares], axis=1)
    for k in (2, 1, 3):
        pltpu.make_async_remote_copy(
            src_ref=dots_in.at[pl.ds(r, 1)],
            dst_ref=dots_in.at[pl.ds(r, 1)],
            send_sem=dot_sem.at[0],
            recv_sem=dot_sem.at[1],
            device_id={"list": l, "row": peer(k)},
            device_id_type=MESH,
        ).start()
    moved = direction[ITERS - 1].astype(F32)
    bend = diag[...][:, :1] * jnp.sum(moved * moved, axis=1, keepdims=True)
    wait_for(last.at[three], last_sem.at[1])
    wait_for(dots_in.at[pl.ds(0, N_ROW - 1)], dot_sem.at[1])
    total = jnp.sum(dots_in[...], axis=0, keepdims=True)[:, :LO]
    total = jnp.sum(jnp.where(square, total, 0.0), axis=1, keepdims=True)
    step_len = last[:, D : D + 1] / (bend + gram_weight * total)
    centroid = last[:, :D] + step_len * moved

    own_rows = pl.ds(pl.multiple_of((c * 2 + zl) * LO, LO), LO)
    pan[own_rows, :] = centroid.astype(BF16)

    def push(j, part, n, device):
        pltpu.make_async_remote_copy(
            src_ref=pan.at[pl.ds(pl.multiple_of((c * 2 + zl) * LO + part * n, n), n)],
            dst_ref=pan.at[pl.ds(pl.multiple_of(((j * 2 + c) * 2 + zl) * LO + part * n, n), n)],
            send_sem=pan_send,
            recv_sem=pan_recv.at[j],
            device_id=device,
            device_id_type=MESH,
        ).start()

    def push_all(j):
        dx, dy = twos[j]
        if j:
            push(j, 0, LO, chip(dx, dy))
        push(j, 0, LO // 2, chip(dx, dy, 1))
        push(j, 1, LO // 2, chip(dx, dy, -1))

    other_core = {"list": list_of(zl, y, x, 1 - c), "row": r}

    def arrive(j):
        wait_for(pan.at[pl.ds(0, 2 * LO if j else LO)], pan_recv.at[j])
        here = pl.ds(pl.multiple_of((j * 2 + c) * 2 * LO, 2 * LO), 2 * LO)
        pltpu.make_async_remote_copy(
            src_ref=pan.at[here],
            dst_ref=pan.at[here],
            send_sem=core_send,
            recv_sem=core_recv.at[j],
            device_id=other_core,
            device_id_type=MESH,
        ).start()

    def score(j, first_block, end_block):
        wide = NEXT_DEV
        chunk = pan[j * 4 * LO : (j + 1) * 4 * LO, :]

        def one(b, carry_):
            lanes = pl.ds(pl.multiple_of(b * wide, wide), wide)
            found = nt(chunk, nexts[lanes, :])
            top = jnp.max(found.reshape(4 * LO // 8, 8, wide), axis=0)
            best[:, lanes] = top if j == 0 else jnp.maximum(best[:, lanes], top)
            return carry_

        lax.fori_loop(first_block, end_block, one, 0)

    for j in range(3):
        push_all(j)
    out_cent[...] = centroid
    arrive(0)
    push_all(3)
    away_end, near_end = AWAY // NEXT_DEV, NEAR // NEXT_DEV
    for j in range(4):
        wait_for(pan.at[pl.ds(0, 2 * LO)], core_recv.at[j])
        if j == 0:
            score(0, away_end, near_end)
            for k in range(4, 12):
                wait_for(nexts.at[pl.ds(0, PIECE)], next_recv.at[k])
        score(j, 0, away_end)
        if j < 3:
            arrive(j + 1)
    for j, (dx, dy) in enumerate(((-1, 0), (1, 0), (0, -1), (0, 1), (-1, -1), (1, 1))):
        best_in[j] = jnp.max(best[:, j * HALF : (j + 1) * HALF], axis=0, keepdims=True)
        pltpu.make_async_remote_copy(
            src_ref=best_in.at[j],
            dst_ref=best_in.at[6 + j],
            send_sem=best_sem.at[0],
            recv_sem=best_sem.at[1],
            device_id=chip(dx, dy),
            device_id_type=MESH,
        ).start()
    for j in range(1, 4):
        score(j, away_end, near_end)
    top_own = jnp.max(best[:, AWAY:], axis=0, keepdims=True)

    wait_for(ids_send.at[pl.ds(0, N_LIST - 1)], ids_send_sem)
    wait_for(send.at[pl.ds(0, (N_LIST - 1) * CAP2)], a2a_send)
    wait_for(nexts.at[pl.ds(0, 12 * PIECE)], next_send)
    wait_for(first_high.at[three], high_sem.at[0])
    wait_for(first_low.at[three], low_sem.at[0])
    for step in range(ITERS):
        wait_for(direction.at[step].at[three], dir_sem.at[2 * step])
    for step in range(ITERS - 1):
        wait_for(grams.at[step].at[three], gram_sem.at[2 * step])
    wait_for(last.at[three], last_sem.at[0])
    wait_for(dots_in.at[pl.ds(0, N_ROW - 1)], dot_sem.at[0])
    wait_for(pan.at[pl.ds(0, 7 * LO)], pan_send)
    wait_for(pan.at[pl.ds(0, 8 * LO)], core_send)
    wait_for(best_in.at[pl.ds(0, 6)], best_sem.at[0])
    wait_for(best_in.at[pl.ds(0, 6)], best_sem.at[1])
    for h in range(2):
        top = top_own[:, h * HALF : (h + 1) * HALF]
        for k in range(3):
            top = jnp.maximum(top, best_in[6 + 2 * k + h])
        out_best[:, h * HALF : (h + 1) * HALF] = top / D


def on_device(corpus, row_list, list_slot, member_counts, old_centroids, next_rows):
    vmem = pl.BlockSpec(memory_space=pltpu.VMEM)
    hbm = pl.BlockSpec(memory_space=pl.ANY)
    dma = pltpu.SemaphoreType.DMA
    cent, best = pl.pallas_call(
        kernel,
        out_shape=(
            jax.ShapeDtypeStruct((LO, D), F32),
            jax.ShapeDtypeStruct((1, NEXT_DEV), F32),
        ),
        in_specs=[hbm, vmem, vmem, vmem, vmem, hbm],
        out_specs=(vmem, vmem),
        scratch_shapes=[
            pltpu.VMEM((ROWS_DEV, D), BF16),
            pltpu.VMEM((N_LIST, ROWS_DEV), I32),
            pltpu.VMEM((N_LIST, 128), F32),
            pltpu.VMEM((N_LIST * CAP2, H), BF16),
            pltpu.VMEM((N_LIST, 128), F32),
            pltpu.VMEM((N_LIST * CAP2, H), BF16),
            pltpu.VMEM((N_LIST * CAP, D), BF16),
            pltpu.VMEM((LO, N_LIST * CAP), F32),
            pltpu.VMEM((LO, D), F32),
            pltpu.VMEM((LO, D), BF16),
            pltpu.VMEM((LO, D), BF16),
            pltpu.VMEM((LO, D), BF16),
            pltpu.VMEM((LO, D), BF16),
            pltpu.VMEM((LO, D), F32),
            pltpu.VMEM((ITERS, LO, D), BF16),
            pltpu.VMEM((ITERS - 1, LO, D), BF16),
            pltpu.VMEM((ITERS - 1, LO, D), BF16),
            pltpu.VMEM((LO, D + 128), F32),
            pltpu.VMEM((N_ROW, 128), F32),
            pltpu.VMEM((LO, 128), F32),
            pltpu.VMEM((SHARDS * LO, D), BF16),
            pltpu.VMEM((NEAR, D), BF16),
            pltpu.VMEM((8, NEAR), F32),
            pltpu.VMEM((12, 1, HALF), F32),
            dma, dma, dma((4,)), dma, dma((4,)),
            dma((2,)), dma((2,)), dma((2 * ITERS,)), dma((2 * ITERS - 2,)), dma((2,)), dma((2,)),
            dma, dma, dma((12,)), dma, dma((4,)), dma, dma((4,)), dma((2,)),
        ],
        compiler_params=pltpu.CompilerParams(
            collective_id=0, has_side_effects=True, vmem_limit_bytes=56 * 2**20
        ),
    )(
        corpus,
        row_list.reshape(1, ROWS_DEV),
        list_slot.reshape(32, 128),
        member_counts.reshape(1, LO),
        old_centroids,
        next_rows,
    )
    return cent, best.reshape(NEXT_DEV)


def solution(mesh):
    in_specs = (
        P(("list", "row"), None),
        P(("list", "row")),
        P(),
        P("list"),
        P("list", None),
        P(("list", "row"), None),
    )
    out_specs = (P("list", None), P(("list", "row")))
    return jax.shard_map(
        on_device, mesh=mesh, in_specs=in_specs, out_specs=out_specs, check_vma=False
    )
```

```python
import itertools

import jax
import jax.numpy as jnp
from jax import lax
from jax.experimental import pallas as pl
from jax.experimental.pallas import tpu as pltpu
from jax.sharding import PartitionSpec as P

MESH = pl.DeviceIdType.MESH
F32 = jnp.float32
BF16 = jnp.bfloat16
I32 = jnp.int32

ITERS = 3
N_LIST = 64
N_ROW = 4
LO = 64
D = 768
H = D // 2
ROWS_DEV = 1024
NEXT_DEV = 1536
CAP = 24
CAP2 = 2 * CAP
GROUP = 16
QUARTER = LO // N_ROW
SHARDS = 16
HALF = NEXT_DEV // 2
PIECE = HALF // 2
AWAY = 6 * HALF
RING = (0, 1, 2, 1)
SEND_ORDER = (1, 3, 2, 0)
NEAR = AWAY + NEXT_DEV

eps_norm = 1e-06
aniso_par = 32.0
perp_weight = 1.0
prior_weight = 16.0
gram_weight = aniso_par - perp_weight


def nt(a, b):
    return lax.dot_general(a, b, (((1,), (1,)), ((), ())), preferred_element_type=F32)


def nn(a, b):
    return lax.dot_general(a, b, (((1,), (0,)), ((), ())), preferred_element_type=F32)


def split_pair(values):
    high_part = values.astype(BF16)
    low_part = (values - high_part.astype(F32)).astype(BF16)
    return high_part, low_part


def iota(shape, dim):
    return lax.broadcasted_iota(I32, shape, dim)


def wait_for(ref, sem):
    pltpu.make_async_copy(ref, ref, sem).wait()


def kernel(
    corpus_hbm, row_list, list_slot, counts, old, next_hbm,
    out_cent, out_best,
    corpus, key, ids_send, send, ids_recv, recv, unit, member,
    first, first_high, first_low, high_in, low_in, gram_all, direction, grams, grams_in,
    last, dots_in, diag, pan, nexts, best, best_in,
    corpus_sem, a2a_send, a2a_recv, ids_send_sem, ids_recv_sem,
    high_sem, low_sem, dir_sem, gram_sem, last_sem, dot_sem,
    next_sem, next_send, next_recv, pan_send, pan_recv, core_send, core_recv, best_sem,
):
    l = lax.axis_index("list")
    r = lax.axis_index("row")
    c = l % 2
    x = (l // 2) % 4
    y = (l // 8) % 4
    zl = l // 32

    def list_of(zl_, y_, x_, c_):
        return ((zl_ * 4 + y_) * 4 + x_) * 2 + c_

    mine = (y - x + 4) % 4
    place = mine * GROUP + zl * 8 + x * 2 + c

    z_part = [zl * 32, (1 - zl) * 32]
    y_part = [((y + k) % 4) * 8 for k in range(4)]
    x_at = [(x + k) % 4 for k in range(4)]
    c_at = [c, 1 - c]

    beyond = (r + 2 * zl - 1 + N_ROW) % N_ROW
    row_core = [r + (beyond - r) * c_at[k] for k in range(2)]
    row_from = [[r, r], row_core]
    row_to = [r, row_core[0]]

    def chip(dx, dy, dz=0):
        spot_ = list_of(zl if dz == 0 else 1 - zl, (y + dy + 4) % 4, (x + dx + 4) % 4, c)
        row = r if dz == 0 else (r + zl + (0 if dz > 0 else N_ROW - 1)) % N_ROW
        return {"list": spot_, "row": row}

    twos = ((0, 0), (2, 0), (0, 2), (2, 2))

    barrier = pltpu.get_barrier_semaphore()

    def greet_device(device):
        pl.semaphore_signal(barrier, inc=1, device_id=device, device_id_type=MESH)

    for k in (2, 1, 3):
        greet_device({"list": l, "row": (r + k) % N_ROW})
    for dx, dy in twos[::-1]:
        for dz in (1, -1):
            greet_device(chip(dx, dy, dz))
    offsets = itertools.product(range(4), range(4), range(2), range(2))
    for dy, dx, dz, dc in sorted(offsets, key=lambda o: -RING[o[0]] - RING[o[1]] - o[2]):
        if dy or dx or dz or dc:
            other = z_part[dz] + y_part[dy] + x_at[dx] * 2 + c_at[dc]
            greet_device({"list": other, "row": row_from[dz][dc]})

    own_corpus = pltpu.make_async_copy(corpus_hbm, corpus, corpus_sem)
    own_corpus.start()
    own_next = pltpu.make_async_copy(next_hbm, nexts.at[pl.ds(AWAY, NEXT_DEV)], next_sem)
    own_next.start()

    ids_row = row_list[...]
    table = list_slot[...]
    table2 = jnp.concatenate([(table // LO) * LO, table % LO], axis=0).astype(F32)
    high = ids_row // 128
    low = ids_row % 128
    pick = (iota((32, ROWS_DEV), 0) == high).astype(F32)
    pick2 = jnp.concatenate([pick, pick], axis=0).astype(BF16)
    looked = nn(table2.T.astype(BF16), pick2)
    slot = jnp.sum(
        jnp.where(iota((128, ROWS_DEV), 0) == low, looked, 0.0), axis=0, keepdims=True
    ).astype(I32)
    owner = slot // LO
    local = slot % LO
    oc = owner % 2
    ox = (owner // 2) % 4
    oy = (owner // 8) % 4
    oz = owner // 32
    spot = ((oy - ox + 4) % 4) * GROUP + oz * 8 + ox * 2 + oc
    hit = iota((N_LIST, ROWS_DEV), 0) == spot
    hits = hit.astype(F32)
    before = (iota((256, 256), 0) < iota((256, 256), 1)).astype(F32).astype(BF16)
    carry = jnp.zeros((N_LIST, 1), F32)
    ranks = []
    for b in range(ROWS_DEV // 256):
        part = hits[:, b * 256 : (b + 1) * 256]
        ranks.append(nn(part.astype(BF16), before) + carry)
        carry = carry + jnp.sum(part, axis=1, keepdims=True)
    rank = jnp.concatenate(ranks, axis=1)
    key[...] = jnp.where(hit, rank, -1.0).astype(I32)
    rank_row = jnp.sum(hits * rank, axis=0, keepdims=True).astype(I32)
    named = (hits * (local + 1).astype(F32)).astype(BF16)
    at_rank = (iota((128, ROWS_DEV), 0) == rank_row).astype(F32).astype(BF16)
    ids_send[...] = nt(named, at_rank) - 1.0

    own_corpus.wait()

    def fill_group(group, carry_):
        keys = key[pl.ds(pl.multiple_of(group * GROUP, GROUP), GROUP), :]
        chosen = keys.reshape(GROUP, 1, ROWS_DEV) == iota((GROUP, CAP, ROWS_DEV), 1)
        chosen = chosen.astype(F32).reshape(GROUP * CAP, ROWS_DEV).astype(BF16)
        rows = nn(chosen, corpus[...]).reshape(GROUP, CAP, D)
        rows = jnp.concatenate([rows[:, :, :H], rows[:, :, H:]], axis=1)
        send[pl.ds(pl.multiple_of(group * GROUP * CAP2, GROUP * CAP2), GROUP * CAP2), :] = (
            rows.reshape(GROUP * CAP2, H).astype(BF16)
        )
        return carry_

    lax.fori_loop(0, 4, fill_group, 0)
    pl.semaphore_wait(barrier, N_LIST - 1 + N_ROW - 1 + 8)

    def send_group(chunk):
        group = (mine + chunk) % 4

        def send_one(to, device):
            pltpu.make_async_remote_copy(
                src_ref=ids_send.at[pl.ds(to, 1)],
                dst_ref=ids_recv.at[pl.ds(place, 1)],
                send_sem=ids_send_sem,
                recv_sem=ids_recv_sem.at[chunk],
                device_id=device,
                device_id_type=MESH,
            ).start()
            pltpu.make_async_remote_copy(
                src_ref=send.at[pl.ds(pl.multiple_of(to * CAP2, CAP2), CAP2)],
                dst_ref=recv.at[pl.ds(pl.multiple_of(place * CAP2, CAP2), CAP2)],
                send_sem=a2a_send,
                recv_sem=a2a_recv.at[chunk],
                device_id=device,
                device_id_type=MESH,
            ).start()

        for dx in SEND_ORDER:
            y_part_ = ((y + dx + chunk) % 4) * 8
            for dz in (1, 0):
                for dc in range(2):
                    to = group * GROUP + z_part[dz] // 4 + x_at[dx] * 2 + c_at[dc]
                    device = {
                        "list": z_part[dz] + y_part_ + x_at[dx] * 2 + c_at[dc],
                        "row": row_to[dz],
                    }
                    if dx or dz or dc:
                        send_one(to, device)
                    else:
                        pl.when(chunk > 0)(lambda to=to, device=device: send_one(to, device))

    def send_next(chunk, carry_):
        send_group(chunk)
        return carry_

    lax.fori_loop(0, 4, send_next, 0)
    own_block = pl.ds(pl.multiple_of(place * CAP2, CAP2), CAP2)
    recv[own_block, :] = send[own_block, :]
    ids_recv[pl.ds(place, 1), :] = ids_send[pl.ds(place, 1), :]

    count_row = counts[...].astype(F32)
    square = iota((LO, LO), 0) == iota((LO, LO), 1)
    count_col = jnp.sum(jnp.where(square, count_row, 0.0), axis=1, keepdims=True)
    diag[...] = jnp.broadcast_to(perp_weight * count_col + prior_weight, (LO, 128))

    def pass_on(start, to_set, part, device, at):
        pltpu.make_async_remote_copy(
            src_ref=nexts.at[pl.ds(start, PIECE)],
            dst_ref=nexts.at[pl.ds(to_set * HALF + part * PIECE, PIECE)],
            send_sem=next_send,
            recv_sem=next_recv.at[at],
            device_id=device,
            device_id_type=MESH,
        ).start()

    sides = ((1, 0), (-1, 0), (0, 1), (0, -1))

    old_high, old_low = split_pair(old[...])
    old_two = jnp.concatenate([old_high, old_low], axis=0)
    width = GROUP * CAP
    source_of = (iota((GROUP, width), 1) * 2731) // 65536
    lane = iota((128, width), 1)
    spread = (lane - ((lane * 2731) // 65536) * CAP == iota((128, width), 0)).astype(F32).astype(BF16)
    first[...] = jnp.zeros_like(first)

    def take_group(chunk, carry_):
        group = (mine - chunk + 4) % 4

        @pl.when(chunk == 0)
        def _():
            wait_for(ids_recv.at[pl.ds(0, GROUP - 1)], ids_recv_sem.at[0])
            wait_for(recv.at[pl.ds(0, (GROUP - 1) * CAP2)], a2a_recv.at[0])

        @pl.when(chunk > 0)
        def _():
            wait_for(ids_recv.at[pl.ds(0, GROUP)], ids_recv_sem.at[chunk])
            wait_for(recv.at[pl.ds(0, GROUP * CAP2)], a2a_recv.at[chunk])

        @pl.when(chunk == 3)
        def _():
            own_next.wait()
            for j, (dx, dy) in enumerate(sides):
                pass_on(AWAY + (j % 2) * HALF + (j // 2) * PIECE, j, j // 2, chip(dx, dy), j)

        named_in = ids_recv[pl.ds(pl.multiple_of(group * GROUP, GROUP), GROUP), :]
        wide = nn(named_in.astype(BF16), spread)
        flat = jnp.sum(
            jnp.where(source_of == iota((GROUP, width), 0), wide, 0.0), axis=0, keepdims=True
        ).astype(I32)
        own = (iota((LO, width), 0) == flat).astype(F32)
        member[:, pl.ds(pl.multiple_of(group * width, width), width)] = own
        raw = recv[pl.ds(pl.multiple_of(group * GROUP * CAP2, GROUP * CAP2), GROUP * CAP2), :]
        raw = raw.astype(F32).reshape(GROUP, CAP2, H)
        rows = jnp.concatenate(
            [raw[:, :CAP, :].reshape(width, H), raw[:, CAP:, :].reshape(width, H)], axis=1
        )
        inverse = lax.rsqrt(jnp.sum(rows * rows, axis=1, keepdims=True) + eps_norm)
        units = (rows * inverse).astype(BF16)
        unit[pl.ds(pl.multiple_of(group * width, width), width), :] = units
        scores = nt(old_two, units)
        scores = (scores[:LO] + scores[LO:]) * own * (-gram_weight)
        wgt_high, wgt_low = split_pair(scores)
        first[...] += (
            nn((own * aniso_par).astype(BF16), rows.astype(BF16))
            + nn(wgt_high, units)
            + nn(wgt_low, units)
        )
        return carry_

    lax.fori_loop(0, 4, take_group, 0)

    quarter = pl.ds(pl.multiple_of(r * QUARTER, QUARTER), QUARTER)

    def peer(k):
        return (r + k) % N_ROW

    def rows_of(k):
        return pl.ds(pl.multiple_of(peer(k) * QUARTER, QUARTER), QUARTER)

    def scatter(source, target, send_sem, recv_sem):
        for k in (2, 1, 3):
            pltpu.make_async_remote_copy(
                src_ref=source.at[rows_of(k)],
                dst_ref=target.at[quarter],
                send_sem=send_sem,
                recv_sem=recv_sem,
                device_id={"list": l, "row": peer(k)},
                device_id_type=MESH,
            ).start()

    def gather(ref, send_sem, recv_sem):
        for k in (2, 1, 3):
            pltpu.make_async_remote_copy(
                src_ref=ref.at[quarter],
                dst_ref=ref.at[quarter],
                send_sem=send_sem,
                recv_sem=recv_sem,
                device_id={"list": l, "row": peer(k)},
                device_id_type=MESH,
            ).start()

    three = pl.ds(0, 3 * QUARTER)

    def pass_more():
        for j in range(4):
            wait_for(nexts.at[pl.ds(0, PIECE)], next_recv.at[j])
        for j, (dx, dy) in enumerate(sides):
            part = j // 2
            over = chip(dy, dx)
            pass_on(j * HALF + part * PIECE, 4 + j % 2, part, over, 8 + j)
            pass_on(AWAY + (j % 2) * HALF + (1 - part) * PIECE, j, 1 - part, chip(dx, dy), 4 + j)

    high_part, low_part = split_pair(first[...])
    first_high[...] = high_part
    first_low[...] = low_part
    scatter(first_high, high_in, high_sem.at[0], high_sem.at[1])
    scatter(first_low, low_in, low_sem.at[0], low_sem.at[1])
    old_own = old[quarter, :]
    diag_own = diag[quarter, :][:, :1]
    residual = first[quarter, :] + (prior_weight - diag_own) * old_own
    wait_for(high_in.at[three], high_sem.at[1])
    for k in range(1, N_ROW):
        residual = residual + high_in[rows_of(k), :].astype(F32)
    centroid = old_own
    moved = residual
    for step in range(ITERS):
        dir_now = direction.at[step]
        dir_now[quarter, :] = moved.astype(BF16)
        moved = moved.astype(BF16).astype(F32)
        gather(dir_now, dir_sem.at[2 * step], dir_sem.at[2 * step + 1])
        if step == ITERS - 1:
            last[quarter, :D] = centroid
            last[quarter, D:] = jnp.broadcast_to(norm_now, (QUARTER, 128))
            gather(last, last_sem.at[0], last_sem.at[1])
        wait_for(dir_now.at[three], dir_sem.at[2 * step + 1])
        scores = nt(dir_now[...], unit[...]) * member[...]
        if step == ITERS - 1:
            break
        gram = nn(scores.astype(BF16), unit[...])
        grams[step] = gram.astype(BF16)
        gram_all[...] = gram
        scatter(
            grams.at[step], grams_in.at[step], gram_sem.at[2 * step], gram_sem.at[2 * step + 1]
        )
        if step == 0:
            pass_more()
            wait_for(low_in.at[three], low_sem.at[1])
            for k in range(1, N_ROW):
                residual = residual + low_in[rows_of(k), :].astype(F32)
            norm_now = jnp.sum(residual * residual, axis=1, keepdims=True)
        wait_for(grams_in.at[step].at[three], gram_sem.at[2 * step + 1])
        total = gram_all[quarter, :]
        for k in range(1, N_ROW):
            total = total + grams_in.at[step][rows_of(k), :].astype(F32)
        applied = diag_own * moved + gram_weight * total
        step_len = norm_now / jnp.sum(moved * applied, axis=1, keepdims=True)
        centroid = centroid + step_len * moved
        residual = residual - step_len * applied
        norm_next = jnp.sum(residual * residual, axis=1, keepdims=True)
        moved = residual + norm_next / norm_now * moved
        norm_now = norm_next

    squares = jnp.sum(scores * scores, axis=1, keepdims=True)
    squares = jnp.sum(jnp.where(square, squares, 0.0), axis=0, keepdims=True)
    dots_in[pl.ds(r, 1), :] = jnp.concatenate([squares, squares], axis=1)
    for k in (2, 1, 3):
        pltpu.make_async_remote_copy(
            src_ref=dots_in.at[pl.ds(r, 1)],
            dst_ref=dots_in.at[pl.ds(r, 1)],
            send_sem=dot_sem.at[0],
            recv_sem=dot_sem.at[1],
            device_id={"list": l, "row": peer(k)},
            device_id_type=MESH,
        ).start()
    moved = direction[ITERS - 1].astype(F32)
    bend = diag[...][:, :1] * jnp.sum(moved * moved, axis=1, keepdims=True)
    wait_for(last.at[three], last_sem.at[1])
    wait_for(dots_in.at[pl.ds(0, N_ROW - 1)], dot_sem.at[1])
    total = jnp.sum(dots_in[...], axis=0, keepdims=True)[:, :LO]
    total = jnp.sum(jnp.where(square, total, 0.0), axis=1, keepdims=True)
    step_len = last[:, D : D + 1] / (bend + gram_weight * total)
    centroid = last[:, :D] + step_len * moved

    def pan_rows(start, n):
        return pl.ds(pl.multiple_of(start, n), n)

    def push(j, part, n, device):
        start = ((j * 2 + c) * 2 + zl) * LO if j else 2 * LO + c * LO
        pltpu.make_async_remote_copy(
            src_ref=pan.at[pan_rows(c * LO + part * n, n)],
            dst_ref=pan.at[pan_rows(start + part * n, n)],
            send_sem=pan_send,
            recv_sem=pan_recv.at[j],
            device_id=device,
            device_id_type=MESH,
        ).start()

    def push_all(j):
        dx, dy = twos[j]
        if j:
            push(j, 0, LO, chip(dx, dy))
        push(j, 0, LO // 2, chip(dx, dy, 1))
        push(j, 1, LO // 2, chip(dx, dy, -1))

    other_core = {"list": list_of(zl, y, x, 1 - c), "row": r}

    def share(rows, at):
        pltpu.make_async_remote_copy(
            src_ref=pan.at[rows],
            dst_ref=pan.at[rows],
            send_sem=core_send,
            recv_sem=core_recv.at[at],
            device_id=other_core,
            device_id_type=MESH,
        ).start()

    def arrive(j):
        n = 2 * LO if j else LO
        wait_for(pan.at[pl.ds(0, n)], pan_recv.at[j])
        share(pan_rows((j * 2 + c) * 2 * LO if j else 2 * LO + c * LO, n), j)

    def score(chunk, first_block, end_block):
        start, end = chunk
        wide = NEXT_DEV
        lists = pan[start:end, :]

        def one(b, carry_):
            lanes = pl.ds(pl.multiple_of(b * wide, wide), wide)
            found = nt(lists, nexts[lanes, :])
            top = jnp.max(found.reshape((end - start) // 8, 8, wide), axis=0)
            best[:, lanes] = jnp.maximum(best[:, lanes], top) if start else top
            return carry_

        lax.fori_loop(first_block, end_block, one, 0)

    own_rows = pan_rows(c * LO, LO)
    pan[own_rows, :] = centroid.astype(BF16)
    share(own_rows, 4)
    for j in range(4):
        push_all(j)
    out_cent[...] = centroid
    away_end, near_end = AWAY // NEXT_DEV, NEAR // NEXT_DEV
    chunks = ((0, 2 * LO), (2 * LO, 8 * LO), (8 * LO, 12 * LO), (12 * LO, 16 * LO))
    wait_for(pan.at[pl.ds(0, LO)], core_recv.at[4])
    score(chunks[0], away_end, near_end)
    arrive(0)
    for k in range(4, 12):
        wait_for(nexts.at[pl.ds(0, PIECE)], next_recv.at[k])
    score(chunks[0], 0, away_end)
    wait_for(pan.at[pl.ds(0, LO)], core_recv.at[0])
    for j in range(1, 4):
        arrive(j)
        wait_for(pan.at[pl.ds(0, 2 * LO)], core_recv.at[j])
        score(chunks[j], 0, away_end)
    for j, (dx, dy) in enumerate(((-1, 0), (1, 0), (0, -1), (0, 1), (-1, -1), (1, 1))):
        best_in[j] = jnp.max(best[:, j * HALF : (j + 1) * HALF], axis=0, keepdims=True)
        pltpu.make_async_remote_copy(
            src_ref=best_in.at[j],
            dst_ref=best_in.at[6 + j],
            send_sem=best_sem.at[0],
            recv_sem=best_sem.at[1],
            device_id=chip(dx, dy),
            device_id_type=MESH,
        ).start()
    for j in range(1, 4):
        score(chunks[j], away_end, near_end)
    top_own = jnp.max(best[:, AWAY:], axis=0, keepdims=True)

    wait_for(ids_send.at[pl.ds(0, N_LIST - 1)], ids_send_sem)
    wait_for(send.at[pl.ds(0, (N_LIST - 1) * CAP2)], a2a_send)
    wait_for(nexts.at[pl.ds(0, 12 * PIECE)], next_send)
    wait_for(first_high.at[three], high_sem.at[0])
    wait_for(first_low.at[three], low_sem.at[0])
    for step in range(ITERS):
        wait_for(direction.at[step].at[three], dir_sem.at[2 * step])
    for step in range(ITERS - 1):
        wait_for(grams.at[step].at[three], gram_sem.at[2 * step])
    wait_for(last.at[three], last_sem.at[0])
    wait_for(dots_in.at[pl.ds(0, N_ROW - 1)], dot_sem.at[0])
    wait_for(pan.at[pl.ds(0, 7 * LO)], pan_send)
    wait_for(pan.at[pl.ds(0, 8 * LO)], core_send)
    wait_for(best_in.at[pl.ds(0, 6)], best_sem.at[0])
    wait_for(best_in.at[pl.ds(0, 6)], best_sem.at[1])
    for h in range(2):
        top = top_own[:, h * HALF : (h + 1) * HALF]
        for k in range(3):
            top = jnp.maximum(top, best_in[6 + 2 * k + h])
        out_best[:, h * HALF : (h + 1) * HALF] = top


def finish(cent, best, out_cent, out_best):
    out_cent[...] = cent[...]
    out_best[...] = best[...].reshape(NEXT_DEV) / D


def on_device(corpus, row_list, list_slot, member_counts, old_centroids, next_rows):
    vmem = pl.BlockSpec(memory_space=pltpu.VMEM)
    hbm = pl.BlockSpec(memory_space=pl.ANY)
    dma = pltpu.SemaphoreType.DMA
    cent, best = pl.pallas_call(
        kernel,
        out_shape=(
            jax.ShapeDtypeStruct((LO, D), F32),
            jax.ShapeDtypeStruct((1, NEXT_DEV), F32),
        ),
        in_specs=[hbm, vmem, vmem, vmem, vmem, hbm],
        out_specs=(vmem, vmem),
        scratch_shapes=[
            pltpu.VMEM((ROWS_DEV, D), BF16),
            pltpu.VMEM((N_LIST, ROWS_DEV), I32),
            pltpu.VMEM((N_LIST, 128), F32),
            pltpu.VMEM((N_LIST * CAP2, H), BF16),
            pltpu.VMEM((N_LIST, 128), F32),
            pltpu.VMEM((N_LIST * CAP2, H), BF16),
            pltpu.VMEM((N_LIST * CAP, D), BF16),
            pltpu.VMEM((LO, N_LIST * CAP), F32),
            pltpu.VMEM((LO, D), F32),
            pltpu.VMEM((LO, D), BF16),
            pltpu.VMEM((LO, D), BF16),
            pltpu.VMEM((LO, D), BF16),
            pltpu.VMEM((LO, D), BF16),
            pltpu.VMEM((LO, D), F32),
            pltpu.VMEM((ITERS, LO, D), BF16),
            pltpu.VMEM((ITERS - 1, LO, D), BF16),
            pltpu.VMEM((ITERS - 1, LO, D), BF16),
            pltpu.VMEM((LO, D + 128), F32),
            pltpu.VMEM((N_ROW, 128), F32),
            pltpu.VMEM((LO, 128), F32),
            pltpu.VMEM((SHARDS * LO, D), BF16),
            pltpu.VMEM((NEAR, D), BF16),
            pltpu.VMEM((8, NEAR), F32),
            pltpu.VMEM((12, 1, HALF), F32),
            dma, dma, dma((4,)), dma, dma((4,)),
            dma((2,)), dma((2,)), dma((2 * ITERS,)), dma((2 * ITERS - 2,)), dma((2,)), dma((2,)),
            dma, dma, dma((12,)), dma, dma((4,)), dma, dma((5,)), dma((2,)),
        ],
        compiler_params=pltpu.CompilerParams(
            collective_id=0, has_side_effects=True, vmem_limit_bytes=56 * 2**20
        ),
    )(
        corpus,
        row_list.reshape(1, ROWS_DEV),
        list_slot.reshape(32, 128),
        member_counts.reshape(1, LO),
        old_centroids,
        next_rows,
    )
    return pl.pallas_call(
        finish,
        out_shape=(
            jax.ShapeDtypeStruct((LO, D), F32),
            jax.ShapeDtypeStruct((NEXT_DEV,), F32),
        ),
        in_specs=[vmem, vmem],
        out_specs=(vmem, vmem),
    )(cent, best)


def solution(mesh):
    in_specs = (
        P(("list", "row"), None),
        P(("list", "row")),
        P(),
        P("list"),
        P("list", None),
        P(("list", "row"), None),
    )
    out_specs = (P("list", None), P(("list", "row")))
    return jax.shard_map(
        on_device, mesh=mesh, in_specs=in_specs, out_specs=out_specs, check_vma=False
    )
```

```python
import itertools

import jax
import jax.numpy as jnp
from jax import lax
from jax.experimental import pallas as pl
from jax.experimental.pallas import tpu as pltpu
from jax.sharding import PartitionSpec as P

MESH = pl.DeviceIdType.MESH
F32 = jnp.float32
BF16 = jnp.bfloat16
I32 = jnp.int32

ITERS = 3
N_LIST = 64
N_ROW = 4
LO = 64
D = 768
H = D // 2
ROWS_DEV = 1024
NEXT_DEV = 1536
CAP = 24
CAP2 = 2 * CAP
GROUP = 16
QUARTER = LO // N_ROW
SHARDS = 16
HALF = NEXT_DEV // 2
PIECE = HALF // 2
AWAY = 6 * HALF
RING = (0, 1, 2, 1)
SEND_ORDER = (1, 3, 2, 0)
NEAR = AWAY + NEXT_DEV

eps_norm = 1e-06
aniso_par = 32.0
perp_weight = 1.0
prior_weight = 16.0
gram_weight = aniso_par - perp_weight


def nt(a, b):
    return lax.dot_general(a, b, (((1,), (1,)), ((), ())), preferred_element_type=F32)


def nn(a, b):
    return lax.dot_general(a, b, (((1,), (0,)), ((), ())), preferred_element_type=F32)


def split_pair(values):
    high_part = values.astype(BF16)
    low_part = (values - high_part.astype(F32)).astype(BF16)
    return high_part, low_part


def iota(shape, dim):
    return lax.broadcasted_iota(I32, shape, dim)


def wait_for(ref, sem):
    pltpu.make_async_copy(ref, ref, sem).wait()


def kernel(
    corpus_hbm, row_list, list_slot, counts, old, next_hbm,
    out_cent, out_best,
    corpus, key, ids_send, send, ids_recv, recv, unit, member,
    first, first_high, first_low, high_in, low_in, gram_all, direction, grams, grams_in,
    last, dots_in, diag, pan, nexts, best, best_in,
    corpus_sem, a2a_send, a2a_recv, ids_send_sem, ids_recv_sem,
    high_sem, low_sem, dir_sem, gram_sem, last_sem, dot_sem,
    next_sem, next_send, next_recv, pan_send, pan_recv, core_send, core_recv, best_sem,
):
    l = lax.axis_index("list")
    r = lax.axis_index("row")
    c = l % 2
    x = (l // 2) % 4
    y = (l // 8) % 4
    zl = l // 32

    def list_of(zl_, y_, x_, c_):
        return ((zl_ * 4 + y_) * 4 + x_) * 2 + c_

    mine = (y - x + 4) % 4
    place = mine * GROUP + zl * 8 + x * 2 + c

    z_part = [zl * 32, (1 - zl) * 32]
    y_part = [((y + k) % 4) * 8 for k in range(4)]
    x_at = [(x + k) % 4 for k in range(4)]
    c_at = [c, 1 - c]

    beyond = (r + 2 * zl - 1 + N_ROW) % N_ROW
    row_core = [r + (beyond - r) * c_at[k] for k in range(2)]
    row_from = [[r, r], row_core]
    row_to = [r, row_core[0]]

    def chip(dx, dy, dz=0):
        spot_ = list_of(zl if dz == 0 else 1 - zl, (y + dy + 4) % 4, (x + dx + 4) % 4, c)
        row = r if dz == 0 else (r + zl + (0 if dz > 0 else N_ROW - 1)) % N_ROW
        return {"list": spot_, "row": row}

    twos = ((0, 0), (2, 0), (0, 2), (2, 2))

    barrier = pltpu.get_barrier_semaphore()

    def greet_device(device):
        pl.semaphore_signal(barrier, inc=1, device_id=device, device_id_type=MESH)

    for k in (2, 1, 3):
        greet_device({"list": l, "row": (r + k) % N_ROW})
    for dx, dy in twos[::-1]:
        greet_device({"list": list_of(1 - zl, (y + dy) % 4, (x + dx) % 4, c), "row": row_core[1]})
    offsets = itertools.product(range(4), range(4), range(2), range(2))
    for dy, dx, dz, dc in sorted(offsets, key=lambda o: -RING[o[0]] - RING[o[1]] - o[2]):
        if dy or dx or dz or dc:
            other = z_part[dz] + y_part[dy] + x_at[dx] * 2 + c_at[dc]
            greet_device({"list": other, "row": row_from[dz][dc]})

    own_corpus = pltpu.make_async_copy(corpus_hbm, corpus, corpus_sem)
    own_corpus.start()
    own_next = pltpu.make_async_copy(next_hbm, nexts.at[pl.ds(AWAY, NEXT_DEV)], next_sem)
    own_next.start()

    ids_row = row_list[...]
    table = list_slot[...]
    table2 = jnp.concatenate([(table // LO) * LO, table % LO], axis=0).astype(F32)
    high = ids_row // 128
    low = ids_row % 128
    pick = (iota((32, ROWS_DEV), 0) == high).astype(F32)
    pick2 = jnp.concatenate([pick, pick], axis=0).astype(BF16)
    looked = nn(table2.T.astype(BF16), pick2)
    slot = jnp.sum(
        jnp.where(iota((128, ROWS_DEV), 0) == low, looked, 0.0), axis=0, keepdims=True
    ).astype(I32)
    owner = slot // LO
    local = slot % LO
    oc = owner % 2
    ox = (owner // 2) % 4
    oy = (owner // 8) % 4
    oz = owner // 32
    spot = ((oy - ox + 4) % 4) * GROUP + oz * 8 + ox * 2 + oc
    hit = iota((N_LIST, ROWS_DEV), 0) == spot
    hits = hit.astype(F32)
    before = (iota((256, 256), 0) < iota((256, 256), 1)).astype(F32).astype(BF16)
    carry = jnp.zeros((N_LIST, 1), F32)
    ranks = []
    for b in range(ROWS_DEV // 256):
        part = hits[:, b * 256 : (b + 1) * 256]
        ranks.append(nn(part.astype(BF16), before) + carry)
        carry = carry + jnp.sum(part, axis=1, keepdims=True)
    rank = jnp.concatenate(ranks, axis=1)
    key[...] = jnp.where(hit, rank, -1.0).astype(I32)
    rank_row = jnp.sum(hits * rank, axis=0, keepdims=True).astype(I32)
    named = (hits * (local + 1).astype(F32)).astype(BF16)
    at_rank = (iota((128, ROWS_DEV), 0) == rank_row).astype(F32).astype(BF16)
    ids_send[...] = nt(named, at_rank) - 1.0

    own_corpus.wait()

    def fill_group(group, carry_):
        keys = key[pl.ds(pl.multiple_of(group * GROUP, GROUP), GROUP), :]
        chosen = keys.reshape(GROUP, 1, ROWS_DEV) == iota((GROUP, CAP, ROWS_DEV), 1)
        chosen = chosen.astype(F32).reshape(GROUP * CAP, ROWS_DEV).astype(BF16)
        rows = nn(chosen, corpus[...]).reshape(GROUP, CAP, D)
        rows = jnp.concatenate([rows[:, :, :H], rows[:, :, H:]], axis=1)
        send[pl.ds(pl.multiple_of(group * GROUP * CAP2, GROUP * CAP2), GROUP * CAP2), :] = (
            rows.reshape(GROUP * CAP2, H).astype(BF16)
        )
        return carry_

    lax.fori_loop(0, 4, fill_group, 0)
    pl.semaphore_wait(barrier, N_LIST - 1 + N_ROW - 1 + len(twos))

    def send_group(chunk):
        group = (mine + chunk) % 4

        def send_one(to, device):
            pltpu.make_async_remote_copy(
                src_ref=ids_send.at[pl.ds(to, 1)],
                dst_ref=ids_recv.at[pl.ds(place, 1)],
                send_sem=ids_send_sem,
                recv_sem=ids_recv_sem.at[chunk],
                device_id=device,
                device_id_type=MESH,
            ).start()
            pltpu.make_async_remote_copy(
                src_ref=send.at[pl.ds(pl.multiple_of(to * CAP2, CAP2), CAP2)],
                dst_ref=recv.at[pl.ds(pl.multiple_of(place * CAP2, CAP2), CAP2)],
                send_sem=a2a_send,
                recv_sem=a2a_recv.at[chunk],
                device_id=device,
                device_id_type=MESH,
            ).start()

        for dx in SEND_ORDER:
            y_part_ = ((y + dx + chunk) % 4) * 8
            for dz in (1, 0):
                for dc in range(2):
                    to = group * GROUP + z_part[dz] // 4 + x_at[dx] * 2 + c_at[dc]
                    device = {
                        "list": z_part[dz] + y_part_ + x_at[dx] * 2 + c_at[dc],
                        "row": row_to[dz],
                    }
                    if dx or dz or dc:
                        send_one(to, device)
                    else:
                        pl.when(chunk > 0)(lambda to=to, device=device: send_one(to, device))

    def send_next(chunk, carry_):
        send_group(chunk)
        return carry_

    lax.fori_loop(0, 4, send_next, 0)
    own_block = pl.ds(pl.multiple_of(place * CAP2, CAP2), CAP2)
    recv[own_block, :] = send[own_block, :]
    ids_recv[pl.ds(place, 1), :] = ids_send[pl.ds(place, 1), :]

    count_row = counts[...].astype(F32)
    square = iota((LO, LO), 0) == iota((LO, LO), 1)
    count_col = jnp.sum(jnp.where(square, count_row, 0.0), axis=1, keepdims=True)
    diag[...] = jnp.broadcast_to(perp_weight * count_col + prior_weight, (LO, 128))

    def pass_on(start, to_set, part, device, at):
        pltpu.make_async_remote_copy(
            src_ref=nexts.at[pl.ds(start, PIECE)],
            dst_ref=nexts.at[pl.ds(to_set * HALF + part * PIECE, PIECE)],
            send_sem=next_send,
            recv_sem=next_recv.at[at],
            device_id=device,
            device_id_type=MESH,
        ).start()

    sides = ((1, 0), (-1, 0), (0, 1), (0, -1))

    old_high, old_low = split_pair(old[...])
    old_two = jnp.concatenate([old_high, old_low], axis=0)
    width = GROUP * CAP
    source_of = (iota((GROUP, width), 1) * 2731) // 65536
    lane = iota((128, width), 1)
    spread = (lane - ((lane * 2731) // 65536) * CAP == iota((128, width), 0)).astype(F32).astype(BF16)
    first[...] = jnp.zeros_like(first)

    def take_group(chunk, carry_):
        group = (mine - chunk + 4) % 4

        @pl.when(chunk == 3)
        def _():
            own_next.wait()
            for j, (dx, dy) in enumerate(sides):
                pass_on(AWAY + (j % 2) * HALF + (j // 2) * PIECE, j, j // 2, chip(dx, dy), j)

        @pl.when(chunk == 0)
        def _():
            wait_for(ids_recv.at[pl.ds(0, GROUP - 1)], ids_recv_sem.at[0])
            wait_for(recv.at[pl.ds(0, (GROUP - 1) * CAP2)], a2a_recv.at[0])

        @pl.when(chunk > 0)
        def _():
            wait_for(ids_recv.at[pl.ds(0, GROUP)], ids_recv_sem.at[chunk])
            wait_for(recv.at[pl.ds(0, GROUP * CAP2)], a2a_recv.at[chunk])

        named_in = ids_recv[pl.ds(pl.multiple_of(group * GROUP, GROUP), GROUP), :]
        wide = nn(named_in.astype(BF16), spread)
        flat = jnp.sum(
            jnp.where(source_of == iota((GROUP, width), 0), wide, 0.0), axis=0, keepdims=True
        ).astype(I32)
        own = (iota((LO, width), 0) == flat).astype(F32)
        member[:, pl.ds(pl.multiple_of(group * width, width), width)] = own
        raw = recv[pl.ds(pl.multiple_of(group * GROUP * CAP2, GROUP * CAP2), GROUP * CAP2), :]
        raw = raw.astype(F32).reshape(GROUP, CAP2, H)
        rows = jnp.concatenate(
            [raw[:, :CAP, :].reshape(width, H), raw[:, CAP:, :].reshape(width, H)], axis=1
        )
        inverse = lax.rsqrt(jnp.sum(rows * rows, axis=1, keepdims=True) + eps_norm)
        units = (rows * inverse).astype(BF16)
        unit[pl.ds(pl.multiple_of(group * width, width), width), :] = units
        scores = nt(old_two, units)
        scores = (scores[:LO] + scores[LO:]) * own * (-gram_weight)
        wgt_high, wgt_low = split_pair(scores)
        first[...] += (
            nn((own * aniso_par).astype(BF16), rows.astype(BF16))
            + nn(wgt_high, units)
            + nn(wgt_low, units)
        )
        return carry_

    lax.fori_loop(0, 4, take_group, 0)

    quarter = pl.ds(pl.multiple_of(r * QUARTER, QUARTER), QUARTER)

    def peer(k):
        return (r + k) % N_ROW

    def rows_of(k):
        return pl.ds(pl.multiple_of(peer(k) * QUARTER, QUARTER), QUARTER)

    def scatter(source, target, send_sem, recv_sem):
        for k in (2, 1, 3):
            pltpu.make_async_remote_copy(
                src_ref=source.at[rows_of(k)],
                dst_ref=target.at[quarter],
                send_sem=send_sem,
                recv_sem=recv_sem,
                device_id={"list": l, "row": peer(k)},
                device_id_type=MESH,
            ).start()

    def gather(ref, send_sem, recv_sem):
        for k in (2, 1, 3):
            pltpu.make_async_remote_copy(
                src_ref=ref.at[quarter],
                dst_ref=ref.at[quarter],
                send_sem=send_sem,
                recv_sem=recv_sem,
                device_id={"list": l, "row": peer(k)},
                device_id_type=MESH,
            ).start()

    three = pl.ds(0, 3 * QUARTER)

    def pass_rest():
        for j, (dx, dy) in enumerate(sides):
            part = 1 - j // 2
            pass_on(AWAY + (j % 2) * HALF + part * PIECE, j, part, chip(dx, dy), 4 + j)

    def pass_over():
        for j in range(4):
            wait_for(nexts.at[pl.ds(0, PIECE)], next_recv.at[j])
        for j, (dx, dy) in enumerate(sides):
            part = j // 2
            pass_on(j * HALF + part * PIECE, 4 + j % 2, part, chip(dy, dx), 8 + j)

    high_part, low_part = split_pair(first[...])
    first_high[...] = high_part
    first_low[...] = low_part
    scatter(first_high, high_in, high_sem.at[0], high_sem.at[1])
    old_own = old[quarter, :]
    diag_own = diag[quarter, :][:, :1]
    residual = first[quarter, :] + (prior_weight - diag_own) * old_own
    wait_for(high_in.at[three], high_sem.at[1])
    pass_rest()
    for k in range(1, N_ROW):
        residual = residual + high_in[rows_of(k), :].astype(F32)
    step_lens = []
    moved = residual
    for step in range(ITERS):
        dir_now = direction.at[step]
        dir_now[quarter, :] = moved.astype(BF16)
        moved = moved.astype(BF16).astype(F32)
        gather(dir_now, dir_sem.at[2 * step], dir_sem.at[2 * step + 1])
        if step == ITERS - 1:
            lane = iota((QUARTER, 128), 1)
            last[quarter, :] = jnp.where(
                lane == 0, step_lens[0], jnp.where(lane == 1, step_lens[1], norm_now)
            )
            gather(last, last_sem.at[0], last_sem.at[1])
        wait_for(dir_now.at[three], dir_sem.at[2 * step + 1])
        if step == 0:
            scatter(first_low, low_in, low_sem.at[0], low_sem.at[1])
        scores = nt(dir_now[...], unit[...]) * member[...]
        if step == ITERS - 1:
            break
        gram = nn(scores.astype(BF16), unit[...])
        grams[step] = gram.astype(BF16)
        gram_all[...] = gram
        scatter(
            grams.at[step], grams_in.at[step], gram_sem.at[2 * step], gram_sem.at[2 * step + 1]
        )
        if step == 0:
            pass_over()
            wait_for(low_in.at[three], low_sem.at[1])
            for k in range(1, N_ROW):
                residual = residual + low_in[rows_of(k), :].astype(F32)
            norm_now = jnp.sum(residual * residual, axis=1, keepdims=True)
        wait_for(grams_in.at[step].at[three], gram_sem.at[2 * step + 1])
        total = gram_all[quarter, :]
        for k in range(1, N_ROW):
            total = total + grams_in.at[step][rows_of(k), :].astype(F32)
        applied = diag_own * moved + gram_weight * total
        step_len = norm_now / jnp.sum(moved * applied, axis=1, keepdims=True)
        step_lens.append(step_len)
        residual = residual - step_len * applied
        norm_next = jnp.sum(residual * residual, axis=1, keepdims=True)
        moved = residual + norm_next / norm_now * moved
        norm_now = norm_next

    squares = jnp.sum(scores * scores, axis=1, keepdims=True)
    squares = jnp.sum(jnp.where(square, squares, 0.0), axis=0, keepdims=True)
    dots_in[pl.ds(r, 1), :] = jnp.concatenate([squares, squares], axis=1)
    for k in (2, 1, 3):
        pltpu.make_async_remote_copy(
            src_ref=dots_in.at[pl.ds(r, 1)],
            dst_ref=dots_in.at[pl.ds(r, 1)],
            send_sem=dot_sem.at[0],
            recv_sem=dot_sem.at[1],
            device_id={"list": l, "row": peer(k)},
            device_id_type=MESH,
        ).start()
    moved = direction[ITERS - 1].astype(F32)
    bend = diag[...][:, :1] * jnp.sum(moved * moved, axis=1, keepdims=True)
    wait_for(last.at[three], last_sem.at[1])
    wait_for(dots_in.at[pl.ds(0, N_ROW - 1)], dot_sem.at[1])
    total = jnp.sum(dots_in[...], axis=0, keepdims=True)[:, :LO]
    total = jnp.sum(jnp.where(square, total, 0.0), axis=1, keepdims=True)
    step_len = last[:, 2:3] / (bend + gram_weight * total)
    centroid = old[...]
    for step in range(ITERS - 1):
        centroid = centroid + last[:, step : step + 1] * direction[step].astype(F32)
    centroid = centroid + step_len * moved

    def pan_rows(start, n):
        return pl.ds(pl.multiple_of(start, n), n)

    def push(j, part, n, device):
        start = ((j * 2 + c) * 2 + zl) * LO if j else 2 * LO + c * LO
        pltpu.make_async_remote_copy(
            src_ref=pan.at[pan_rows(c * LO + part * n, n)],
            dst_ref=pan.at[pan_rows(start + part * n, n)],
            send_sem=pan_send,
            recv_sem=pan_recv.at[j],
            device_id=device,
            device_id_type=MESH,
        ).start()

    def push_all(j):
        dx, dy = twos[j]
        if j:
            push(j, 0, LO, chip(dx, dy))
        push(j, 0, LO // 2, chip(dx, dy, 1))
        push(j, 1, LO // 2, chip(dx, dy, -1))

    other_core = {"list": list_of(zl, y, x, 1 - c), "row": r}

    def share(rows, at):
        pltpu.make_async_remote_copy(
            src_ref=pan.at[rows],
            dst_ref=pan.at[rows],
            send_sem=core_send,
            recv_sem=core_recv.at[at],
            device_id=other_core,
            device_id_type=MESH,
        ).start()

    def arrive(j):
        n = 2 * LO if j else LO
        wait_for(pan.at[pl.ds(0, n)], pan_recv.at[j])
        share(pan_rows((j * 2 + c) * 2 * LO if j else 2 * LO + c * LO, n), j)

    def score(chunk, first_block, end_block):
        start, end = chunk
        wide = NEXT_DEV
        lists = pan[start:end, :]

        def one(b, carry_):
            lanes = pl.ds(pl.multiple_of(b * wide, wide), wide)
            found = nt(lists, nexts[lanes, :])
            top = jnp.max(found.reshape((end - start) // 8, 8, wide), axis=0)
            best[:, lanes] = jnp.maximum(best[:, lanes], top) if start else top
            return carry_

        lax.fori_loop(first_block, end_block, one, 0)

    own_rows = pan_rows(c * LO, LO)
    pan[own_rows, :] = centroid.astype(BF16)
    share(own_rows, 4)
    for j in range(4):
        push_all(j)
    out_cent[...] = centroid
    away_end, near_end = AWAY // NEXT_DEV, NEAR // NEXT_DEV
    chunks = ((0, 2 * LO), (2 * LO, 8 * LO), (8 * LO, 12 * LO), (12 * LO, 16 * LO))
    wait_for(pan.at[pl.ds(0, LO)], core_recv.at[4])
    score(chunks[0], away_end, near_end)
    arrive(0)
    for k in range(4, 12):
        wait_for(nexts.at[pl.ds(0, PIECE)], next_recv.at[k])
    score(chunks[0], 0, away_end)
    wait_for(pan.at[pl.ds(0, LO)], core_recv.at[0])
    for j in range(1, 4):
        arrive(j)
        wait_for(pan.at[pl.ds(0, 2 * LO)], core_recv.at[j])
        score(chunks[j], 0, away_end)
    for j, (dx, dy) in enumerate(((-1, 0), (1, 0), (0, -1), (0, 1), (-1, -1), (1, 1))):
        best_in[j] = jnp.max(best[:, j * HALF : (j + 1) * HALF], axis=0, keepdims=True)
        pltpu.make_async_remote_copy(
            src_ref=best_in.at[j],
            dst_ref=best_in.at[6 + j],
            send_sem=best_sem.at[0],
            recv_sem=best_sem.at[1],
            device_id=chip(dx, dy),
            device_id_type=MESH,
        ).start()
    for j in range(1, 4):
        score(chunks[j], away_end, near_end)
    top_own = jnp.max(best[:, AWAY:], axis=0, keepdims=True)

    wait_for(ids_send.at[pl.ds(0, N_LIST - 1)], ids_send_sem)
    wait_for(send.at[pl.ds(0, (N_LIST - 1) * CAP2)], a2a_send)
    wait_for(nexts.at[pl.ds(0, 12 * PIECE)], next_send)
    wait_for(first_high.at[three], high_sem.at[0])
    wait_for(first_low.at[three], low_sem.at[0])
    for step in range(ITERS):
        wait_for(direction.at[step].at[three], dir_sem.at[2 * step])
    for step in range(ITERS - 1):
        wait_for(grams.at[step].at[three], gram_sem.at[2 * step])
    wait_for(last.at[three], last_sem.at[0])
    wait_for(dots_in.at[pl.ds(0, N_ROW - 1)], dot_sem.at[0])
    wait_for(pan.at[pl.ds(0, 7 * LO)], pan_send)
    wait_for(pan.at[pl.ds(0, 8 * LO)], core_send)
    wait_for(best_in.at[pl.ds(0, 6)], best_sem.at[0])
    wait_for(best_in.at[pl.ds(0, 6)], best_sem.at[1])
    for h in range(2):
        top = top_own[:, h * HALF : (h + 1) * HALF]
        for k in range(3):
            top = jnp.maximum(top, best_in[6 + 2 * k + h])
        out_best[:, h * HALF : (h + 1) * HALF] = top


def finish(cent, best, out_cent, out_best):
    out_cent[...] = cent[...]
    out_best[...] = best[...].reshape(NEXT_DEV) / D


def on_device(corpus, row_list, list_slot, member_counts, old_centroids, next_rows):
    vmem = pl.BlockSpec(memory_space=pltpu.VMEM)
    hbm = pl.BlockSpec(memory_space=pl.ANY)
    dma = pltpu.SemaphoreType.DMA
    cent, best = pl.pallas_call(
        kernel,
        out_shape=(
            jax.ShapeDtypeStruct((LO, D), F32),
            jax.ShapeDtypeStruct((1, NEXT_DEV), F32),
        ),
        in_specs=[hbm, vmem, vmem, vmem, vmem, hbm],
        out_specs=(vmem, vmem),
        scratch_shapes=[
            pltpu.VMEM((ROWS_DEV, D), BF16),
            pltpu.VMEM((N_LIST, ROWS_DEV), I32),
            pltpu.VMEM((N_LIST, 128), F32),
            pltpu.VMEM((N_LIST * CAP2, H), BF16),
            pltpu.VMEM((N_LIST, 128), F32),
            pltpu.VMEM((N_LIST * CAP2, H), BF16),
            pltpu.VMEM((N_LIST * CAP, D), BF16),
            pltpu.VMEM((LO, N_LIST * CAP), F32),
            pltpu.VMEM((LO, D), F32),
            pltpu.VMEM((LO, D), BF16),
            pltpu.VMEM((LO, D), BF16),
            pltpu.VMEM((LO, D), BF16),
            pltpu.VMEM((LO, D), BF16),
            pltpu.VMEM((LO, D), F32),
            pltpu.VMEM((ITERS, LO, D), BF16),
            pltpu.VMEM((ITERS - 1, LO, D), BF16),
            pltpu.VMEM((ITERS - 1, LO, D), BF16),
            pltpu.VMEM((LO, 128), F32),
            pltpu.VMEM((N_ROW, 128), F32),
            pltpu.VMEM((LO, 128), F32),
            pltpu.VMEM((SHARDS * LO, D), BF16),
            pltpu.VMEM((NEAR, D), BF16),
            pltpu.VMEM((8, NEAR), F32),
            pltpu.VMEM((12, 1, HALF), F32),
            dma, dma, dma((4,)), dma, dma((4,)),
            dma((2,)), dma((2,)), dma((2 * ITERS,)), dma((2 * ITERS - 2,)), dma((2,)), dma((2,)),
            dma, dma, dma((12,)), dma, dma((4,)), dma, dma((5,)), dma((2,)),
        ],
        compiler_params=pltpu.CompilerParams(
            collective_id=0, has_side_effects=True, vmem_limit_bytes=56 * 2**20
        ),
    )(
        corpus,
        row_list.reshape(1, ROWS_DEV),
        list_slot.reshape(32, 128),
        member_counts.reshape(1, LO),
        old_centroids,
        next_rows,
    )
    return pl.pallas_call(
        finish,
        out_shape=(
            jax.ShapeDtypeStruct((LO, D), F32),
            jax.ShapeDtypeStruct((NEXT_DEV,), F32),
        ),
        in_specs=[vmem, vmem],
        out_specs=(vmem, vmem),
    )(cent, best)


def solution(mesh):
    in_specs = (
        P(("list", "row"), None),
        P(("list", "row")),
        P(),
        P("list"),
        P("list", None),
        P(("list", "row"), None),
    )
    out_specs = (P("list", None), P(("list", "row")))
    return jax.shard_map(
        on_device, mesh=mesh, in_specs=in_specs, out_specs=out_specs, check_vma=False
    )
```

```python
import itertools

import jax
import jax.numpy as jnp
from jax import lax
from jax.experimental import pallas as pl
from jax.experimental.pallas import tpu as pltpu
from jax.sharding import PartitionSpec as P

MESH = pl.DeviceIdType.MESH
F32 = jnp.float32
BF16 = jnp.bfloat16
I32 = jnp.int32

ITERS = 3
N_LIST = 64
N_ROW = 4
LO = 64
D = 768
H = D // 2
ROWS_DEV = 1024
NEXT_DEV = 1536
CAP = 24
CAP2 = 2 * CAP
GROUP = 16
QUARTER = LO // N_ROW
SHARDS = 16
HALF = NEXT_DEV // 2
PIECE = HALF // 2
AWAY = 6 * HALF
RING = (0, 1, 2, 1)
SEND_ORDER = (1, 3, 2, 0)
NEAR = AWAY + NEXT_DEV

eps_norm = 1e-06
aniso_par = 32.0
perp_weight = 1.0
prior_weight = 16.0
gram_weight = aniso_par - perp_weight


def nt(a, b):
    return lax.dot_general(a, b, (((1,), (1,)), ((), ())), preferred_element_type=F32)


def nn(a, b):
    return lax.dot_general(a, b, (((1,), (0,)), ((), ())), preferred_element_type=F32)


def split_pair(values):
    high_part = values.astype(BF16)
    low_part = (values - high_part.astype(F32)).astype(BF16)
    return high_part, low_part


def iota(shape, dim):
    return lax.broadcasted_iota(I32, shape, dim)


def wait_for(ref, sem):
    pltpu.make_async_copy(ref, ref, sem).wait()


def kernel(
    corpus_hbm, row_list, list_slot, counts, old, next_hbm,
    out_cent, out_best,
    corpus, key, ids_send, send, ids_recv, recv, unit, member,
    first, first_high, first_low, high_in, low_in, gram_all, direction, grams, grams_in,
    last, dots_in, diag, pan, nexts, best, best_in,
    corpus_sem, a2a_send, a2a_recv, ids_send_sem, ids_recv_sem,
    high_sem, low_sem, dir_sem, gram_sem, last_sem, dot_sem,
    next_sem, next_send, next_recv, pan_send, pan_recv, core_send, core_recv, best_sem,
):
    l = lax.axis_index("list")
    r = lax.axis_index("row")
    c = l % 2
    x = (l // 2) % 4
    y = (l // 8) % 4
    zl = l // 32

    def list_of(zl_, y_, x_, c_):
        return ((zl_ * 4 + y_) * 4 + x_) * 2 + c_

    mine = (y - x + 4) % 4
    place = mine * GROUP + zl * 8 + x * 2 + c

    z_part = [zl * 32, (1 - zl) * 32]
    y_part = [((y + k) % 4) * 8 for k in range(4)]
    x_at = [(x + k) % 4 for k in range(4)]
    c_at = [c, 1 - c]

    beyond = (r + 2 * zl - 1 + N_ROW) % N_ROW
    row_core = [r + (beyond - r) * c_at[k] for k in range(2)]
    row_from = [[r, r], row_core]
    row_to = [r, row_core[0]]

    def chip(dx, dy, dz=0):
        spot_ = list_of(zl if dz == 0 else 1 - zl, (y + dy + 4) % 4, (x + dx + 4) % 4, c)
        row = r if dz == 0 else (r + zl + (0 if dz > 0 else N_ROW - 1)) % N_ROW
        return {"list": spot_, "row": row}

    twos = ((0, 0), (2, 0), (0, 2), (2, 2))

    barrier = pltpu.get_barrier_semaphore()

    def greet_device(device):
        pl.semaphore_signal(barrier, inc=1, device_id=device, device_id_type=MESH)

    for k in (2, 1, 3):
        greet_device({"list": l, "row": (r + k) % N_ROW})
    for dx, dy in twos[::-1]:
        greet_device({"list": list_of(1 - zl, (y + dy) % 4, (x + dx) % 4, c), "row": row_core[1]})
    offsets = itertools.product(range(4), range(4), range(2), range(2))
    for dy, dx, dz, dc in sorted(offsets, key=lambda o: -RING[o[0]] - RING[o[1]] - o[2]):
        if dy or dx or dz or dc:
            other = z_part[dz] + y_part[dy] + x_at[dx] * 2 + c_at[dc]
            greet_device({"list": other, "row": row_from[dz][dc]})

    own_corpus = pltpu.make_async_copy(corpus_hbm, corpus, corpus_sem)
    own_corpus.start()
    own_next = pltpu.make_async_copy(next_hbm, nexts.at[pl.ds(AWAY, NEXT_DEV)], next_sem)
    own_next.start()

    ids_row = row_list[...]
    table = list_slot[...]
    table2 = jnp.concatenate([(table // LO) * LO, table % LO], axis=0).astype(F32)
    high = ids_row // 128
    low = ids_row % 128
    pick = (iota((32, ROWS_DEV), 0) == high).astype(F32)
    pick2 = jnp.concatenate([pick, pick], axis=0).astype(BF16)
    looked = nn(table2.T.astype(BF16), pick2)
    slot = jnp.sum(
        jnp.where(iota((128, ROWS_DEV), 0) == low, looked, 0.0), axis=0, keepdims=True
    ).astype(I32)
    owner = slot // LO
    local = slot % LO
    oc = owner % 2
    ox = (owner // 2) % 4
    oy = (owner // 8) % 4
    oz = owner // 32
    spot = ((oy - ox + 4) % 4) * GROUP + oz * 8 + ox * 2 + oc
    hit = iota((N_LIST, ROWS_DEV), 0) == spot
    hits = hit.astype(F32)
    before = (iota((256, 256), 0) < iota((256, 256), 1)).astype(F32).astype(BF16)
    carry = jnp.zeros((N_LIST, 1), F32)
    ranks = []
    for b in range(ROWS_DEV // 256):
        part = hits[:, b * 256 : (b + 1) * 256]
        ranks.append(nn(part.astype(BF16), before) + carry)
        carry = carry + jnp.sum(part, axis=1, keepdims=True)
    rank = jnp.concatenate(ranks, axis=1)
    key[...] = jnp.where(hit, rank, -1.0).astype(I32)
    rank_row = jnp.sum(hits * rank, axis=0, keepdims=True).astype(I32)
    named = (hits * (local + 1).astype(F32)).astype(BF16)
    at_rank = (iota((128, ROWS_DEV), 0) == rank_row).astype(F32).astype(BF16)
    ids_send[...] = nt(named, at_rank) - 1.0

    own_corpus.wait()

    def fill_group(group, carry_):
        keys = key[pl.ds(pl.multiple_of(group * GROUP, GROUP), GROUP), :]
        chosen = keys.reshape(GROUP, 1, ROWS_DEV) == iota((GROUP, CAP, ROWS_DEV), 1)
        chosen = chosen.astype(F32).reshape(GROUP * CAP, ROWS_DEV).astype(BF16)
        rows = nn(chosen, corpus[...]).reshape(GROUP, CAP, D)
        rows = jnp.concatenate([rows[:, :, :H], rows[:, :, H:]], axis=1)
        send[pl.ds(pl.multiple_of(group * GROUP * CAP2, GROUP * CAP2), GROUP * CAP2), :] = (
            rows.reshape(GROUP * CAP2, H).astype(BF16)
        )
        return carry_

    lax.fori_loop(0, 4, fill_group, 0)
    pl.semaphore_wait(barrier, N_LIST - 1 + N_ROW - 1 + len(twos))

    def send_group(chunk):
        group = (mine + chunk) % 4

        def send_one(to, device):
            pltpu.make_async_remote_copy(
                src_ref=ids_send.at[pl.ds(to, 1)],
                dst_ref=ids_recv.at[pl.ds(place, 1)],
                send_sem=ids_send_sem,
                recv_sem=ids_recv_sem.at[chunk],
                device_id=device,
                device_id_type=MESH,
            ).start()
            pltpu.make_async_remote_copy(
                src_ref=send.at[pl.ds(pl.multiple_of(to * CAP2, CAP2), CAP2)],
                dst_ref=recv.at[pl.ds(pl.multiple_of(place * CAP2, CAP2), CAP2)],
                send_sem=a2a_send,
                recv_sem=a2a_recv.at[chunk],
                device_id=device,
                device_id_type=MESH,
            ).start()

        for dx in SEND_ORDER:
            y_part_ = ((y + dx + chunk) % 4) * 8
            for dz in (1, 0):
                for dc in range(2):
                    to = group * GROUP + z_part[dz] // 4 + x_at[dx] * 2 + c_at[dc]
                    device = {
                        "list": z_part[dz] + y_part_ + x_at[dx] * 2 + c_at[dc],
                        "row": row_to[dz],
                    }
                    if dx or dz or dc:
                        send_one(to, device)
                    else:
                        pl.when(chunk > 0)(lambda to=to, device=device: send_one(to, device))

    def send_next(chunk, carry_):
        send_group(chunk)
        return carry_

    lax.fori_loop(0, 4, send_next, 0)
    own_block = pl.ds(pl.multiple_of(place * CAP2, CAP2), CAP2)
    recv[own_block, :] = send[own_block, :]
    ids_recv[pl.ds(place, 1), :] = ids_send[pl.ds(place, 1), :]

    count_row = counts[...].astype(F32)
    square = iota((LO, LO), 0) == iota((LO, LO), 1)
    count_col = jnp.sum(jnp.where(square, count_row, 0.0), axis=1, keepdims=True)
    diag[...] = jnp.broadcast_to(perp_weight * count_col + prior_weight, (LO, 128))

    def pass_on(start, to_set, part, device, at):
        pltpu.make_async_remote_copy(
            src_ref=nexts.at[pl.ds(start, PIECE)],
            dst_ref=nexts.at[pl.ds(to_set * HALF + part * PIECE, PIECE)],
            send_sem=next_send,
            recv_sem=next_recv.at[at],
            device_id=device,
            device_id_type=MESH,
        ).start()

    sides = ((1, 0), (-1, 0), (0, 1), (0, -1))

    old_high, old_low = split_pair(old[...])
    old_two = jnp.concatenate([old_high, old_low], axis=0)
    width = GROUP * CAP
    source_of = (iota((GROUP, width), 1) * 2731) // 65536
    lane = iota((128, width), 1)
    spread = (lane - ((lane * 2731) // 65536) * CAP == iota((128, width), 0)).astype(F32).astype(BF16)
    first[...] = jnp.zeros_like(first)

    def take_group(chunk, carry_):
        group = (mine - chunk + 4) % 4

        @pl.when(chunk == 2)
        def _():
            own_next.wait()
            for j, (dx, dy) in enumerate(sides):
                pass_on(AWAY + (j % 2) * HALF + (j // 2) * PIECE, j, j // 2, chip(dx, dy), j)

        @pl.when(chunk == 0)
        def _():
            wait_for(ids_recv.at[pl.ds(0, GROUP - 1)], ids_recv_sem.at[0])
            wait_for(recv.at[pl.ds(0, (GROUP - 1) * CAP2)], a2a_recv.at[0])

        @pl.when(chunk > 0)
        def _():
            wait_for(ids_recv.at[pl.ds(0, GROUP)], ids_recv_sem.at[chunk])
            wait_for(recv.at[pl.ds(0, GROUP * CAP2)], a2a_recv.at[chunk])

        named_in = ids_recv[pl.ds(pl.multiple_of(group * GROUP, GROUP), GROUP), :]
        wide = nn(named_in.astype(BF16), spread)
        flat = jnp.sum(
            jnp.where(source_of == iota((GROUP, width), 0), wide, 0.0), axis=0, keepdims=True
        ).astype(I32)
        own = (iota((LO, width), 0) == flat).astype(F32)
        member[:, pl.ds(pl.multiple_of(group * width, width), width)] = own
        raw = recv[pl.ds(pl.multiple_of(group * GROUP * CAP2, GROUP * CAP2), GROUP * CAP2), :]
        raw = raw.astype(F32).reshape(GROUP, CAP2, H)
        rows = jnp.concatenate(
            [raw[:, :CAP, :].reshape(width, H), raw[:, CAP:, :].reshape(width, H)], axis=1
        )
        inverse = lax.rsqrt(jnp.sum(rows * rows, axis=1, keepdims=True) + eps_norm)
        units = (rows * inverse).astype(BF16)
        unit[pl.ds(pl.multiple_of(group * width, width), width), :] = units
        scores = nt(old_two, units)
        scores = (scores[:LO] + scores[LO:]) * own * (-gram_weight)
        wgt_high, wgt_low = split_pair(scores)
        first[...] += (
            nn((own * aniso_par).astype(BF16), rows.astype(BF16))
            + nn(wgt_high, units)
            + nn(wgt_low, units)
        )
        return carry_

    lax.fori_loop(0, 4, take_group, 0)

    quarter = pl.ds(pl.multiple_of(r * QUARTER, QUARTER), QUARTER)

    def peer(k):
        return (r + k) % N_ROW

    def rows_of(k):
        return pl.ds(pl.multiple_of(peer(k) * QUARTER, QUARTER), QUARTER)

    def scatter(source, target, send_sem, recv_sem):
        for k in (2, 1, 3):
            pltpu.make_async_remote_copy(
                src_ref=source.at[rows_of(k)],
                dst_ref=target.at[quarter],
                send_sem=send_sem,
                recv_sem=recv_sem,
                device_id={"list": l, "row": peer(k)},
                device_id_type=MESH,
            ).start()

    def gather(ref, send_sem, recv_sem):
        for k in (2, 1, 3):
            pltpu.make_async_remote_copy(
                src_ref=ref.at[quarter],
                dst_ref=ref.at[quarter],
                send_sem=send_sem,
                recv_sem=recv_sem,
                device_id={"list": l, "row": peer(k)},
                device_id_type=MESH,
            ).start()

    three = pl.ds(0, 3 * QUARTER)

    def pass_rest():
        for j, (dx, dy) in enumerate(sides):
            part = 1 - j // 2
            pass_on(AWAY + (j % 2) * HALF + part * PIECE, j, part, chip(dx, dy), 4 + j)

    def pass_over():
        for j in range(4):
            wait_for(nexts.at[pl.ds(0, PIECE)], next_recv.at[j])
        for j, (dx, dy) in enumerate(sides):
            part = j // 2
            pass_on(j * HALF + part * PIECE, 4 + j % 2, part, chip(dy, dx), 8 + j)

    high_part, low_part = split_pair(first[...])
    first_high[...] = high_part
    first_low[...] = low_part
    scatter(first_high, high_in, high_sem.at[0], high_sem.at[1])
    old_own = old[quarter, :]
    diag_own = diag[quarter, :][:, :1]
    residual = first[quarter, :] + (prior_weight - diag_own) * old_own
    wait_for(high_in.at[three], high_sem.at[1])
    pass_rest()
    for k in range(1, N_ROW):
        residual = residual + high_in[rows_of(k), :].astype(F32)
    step_lens = []
    moved = residual
    for step in range(ITERS):
        dir_now = direction.at[step]
        dir_now[quarter, :] = moved.astype(BF16)
        moved = moved.astype(BF16).astype(F32)
        gather(dir_now, dir_sem.at[2 * step], dir_sem.at[2 * step + 1])
        if step == ITERS - 1:
            lane = iota((QUARTER, 128), 1)
            last[quarter, :] = jnp.where(
                lane == 0, step_lens[0], jnp.where(lane == 1, step_lens[1], norm_now)
            )
            gather(last, last_sem.at[0], last_sem.at[1])
        wait_for(dir_now.at[three], dir_sem.at[2 * step + 1])
        if step == 0:
            scatter(first_low, low_in, low_sem.at[0], low_sem.at[1])
        scores = nt(dir_now[...], unit[...]) * member[...]
        if step == ITERS - 1:
            break
        gram = nn(scores.astype(BF16), unit[...])
        grams[step] = gram.astype(BF16)
        gram_all[...] = gram
        scatter(
            grams.at[step], grams_in.at[step], gram_sem.at[2 * step], gram_sem.at[2 * step + 1]
        )
        if step == 0:
            pass_over()
            wait_for(low_in.at[three], low_sem.at[1])
            for k in range(1, N_ROW):
                residual = residual + low_in[rows_of(k), :].astype(F32)
            norm_now = jnp.sum(residual * residual, axis=1, keepdims=True)
        wait_for(grams_in.at[step].at[three], gram_sem.at[2 * step + 1])
        total = gram_all[quarter, :]
        for k in range(1, N_ROW):
            total = total + grams_in.at[step][rows_of(k), :].astype(F32)
        applied = diag_own * moved + gram_weight * total
        step_len = norm_now / jnp.sum(moved * applied, axis=1, keepdims=True)
        step_lens.append(step_len)
        residual = residual - step_len * applied
        norm_next = jnp.sum(residual * residual, axis=1, keepdims=True)
        moved = residual + norm_next / norm_now * moved
        norm_now = norm_next

    squares = jnp.sum(scores * scores, axis=1, keepdims=True)
    squares = jnp.sum(jnp.where(square, squares, 0.0), axis=0, keepdims=True)
    dots_in[pl.ds(r, 1), :] = jnp.concatenate([squares, squares], axis=1)
    for k in (2, 1, 3):
        pltpu.make_async_remote_copy(
            src_ref=dots_in.at[pl.ds(r, 1)],
            dst_ref=dots_in.at[pl.ds(r, 1)],
            send_sem=dot_sem.at[0],
            recv_sem=dot_sem.at[1],
            device_id={"list": l, "row": peer(k)},
            device_id_type=MESH,
        ).start()
    moved = direction[ITERS - 1].astype(F32)
    bend = diag[...][:, :1] * jnp.sum(moved * moved, axis=1, keepdims=True)
    wait_for(last.at[three], last_sem.at[1])
    wait_for(dots_in.at[pl.ds(0, N_ROW - 1)], dot_sem.at[1])
    total = jnp.sum(dots_in[...], axis=0, keepdims=True)[:, :LO]
    total = jnp.sum(jnp.where(square, total, 0.0), axis=1, keepdims=True)
    step_len = last[:, 2:3] / (bend + gram_weight * total)
    centroid = old[...]
    for step in range(ITERS - 1):
        centroid = centroid + last[:, step : step + 1] * direction[step].astype(F32)
    centroid = centroid + step_len * moved

    def pan_rows(start, n):
        return pl.ds(pl.multiple_of(start, n), n)

    def push(j, part, n, device):
        start = ((j * 2 + c) * 2 + zl) * LO if j else 2 * LO + c * LO
        pltpu.make_async_remote_copy(
            src_ref=pan.at[pan_rows(c * LO + part * n, n)],
            dst_ref=pan.at[pan_rows(start + part * n, n)],
            send_sem=pan_send,
            recv_sem=pan_recv.at[j],
            device_id=device,
            device_id_type=MESH,
        ).start()

    def push_all(j):
        dx, dy = twos[j]
        if j:
            push(j, 0, LO, chip(dx, dy))
        push(j, 0, LO // 2, chip(dx, dy, 1))
        push(j, 1, LO // 2, chip(dx, dy, -1))

    other_core = {"list": list_of(zl, y, x, 1 - c), "row": r}

    def share(rows, at):
        pltpu.make_async_remote_copy(
            src_ref=pan.at[rows],
            dst_ref=pan.at[rows],
            send_sem=core_send,
            recv_sem=core_recv.at[at],
            device_id=other_core,
            device_id_type=MESH,
        ).start()

    def arrive(j):
        n = 2 * LO if j else LO
        wait_for(pan.at[pl.ds(0, n)], pan_recv.at[j])
        share(pan_rows((j * 2 + c) * 2 * LO if j else 2 * LO + c * LO, n), j)

    def score(chunk, first_block, end_block):
        start, end = chunk
        wide = NEXT_DEV
        lists = pan[start:end, :]

        def one(b, carry_):
            lanes = pl.ds(pl.multiple_of(b * wide, wide), wide)
            found = nt(lists, nexts[lanes, :])
            top = jnp.max(found.reshape((end - start) // 8, 8, wide), axis=0)
            best[:, lanes] = jnp.maximum(best[:, lanes], top) if start else top
            return carry_

        lax.fori_loop(first_block, end_block, one, 0)

    own_rows = pan_rows(c * LO, LO)
    pan[own_rows, :] = centroid.astype(BF16)
    share(own_rows, 4)
    for j in range(4):
        push_all(j)
    out_cent[...] = centroid
    away_end, near_end = AWAY // NEXT_DEV, NEAR // NEXT_DEV
    chunks = ((0, 2 * LO), (2 * LO, 8 * LO), (8 * LO, 12 * LO), (12 * LO, 16 * LO))
    wait_for(pan.at[pl.ds(0, LO)], core_recv.at[4])
    score(chunks[0], away_end, near_end)
    arrive(0)
    for k in range(4, 12):
        wait_for(nexts.at[pl.ds(0, PIECE)], next_recv.at[k])
    score(chunks[0], 0, away_end)
    wait_for(pan.at[pl.ds(0, LO)], core_recv.at[0])
    for j in range(1, 4):
        arrive(j)
        wait_for(pan.at[pl.ds(0, 2 * LO)], core_recv.at[j])
        score(chunks[j], 0, away_end)
    for j, (dx, dy) in enumerate(((-1, 0), (1, 0), (0, -1), (0, 1), (-1, -1), (1, 1))):
        best_in[j] = jnp.max(best[:, j * HALF : (j + 1) * HALF], axis=0, keepdims=True)
        pltpu.make_async_remote_copy(
            src_ref=best_in.at[j],
            dst_ref=best_in.at[6 + j],
            send_sem=best_sem.at[0],
            recv_sem=best_sem.at[1],
            device_id=chip(dx, dy),
            device_id_type=MESH,
        ).start()
    for j in range(1, 4):
        score(chunks[j], away_end, near_end)
    top_own = jnp.max(best[:, AWAY:], axis=0, keepdims=True)

    wait_for(ids_send.at[pl.ds(0, N_LIST - 1)], ids_send_sem)
    wait_for(send.at[pl.ds(0, (N_LIST - 1) * CAP2)], a2a_send)
    wait_for(nexts.at[pl.ds(0, 12 * PIECE)], next_send)
    wait_for(first_high.at[three], high_sem.at[0])
    wait_for(first_low.at[three], low_sem.at[0])
    for step in range(ITERS):
        wait_for(direction.at[step].at[three], dir_sem.at[2 * step])
    for step in range(ITERS - 1):
        wait_for(grams.at[step].at[three], gram_sem.at[2 * step])
    wait_for(last.at[three], last_sem.at[0])
    wait_for(dots_in.at[pl.ds(0, N_ROW - 1)], dot_sem.at[0])
    wait_for(pan.at[pl.ds(0, 7 * LO)], pan_send)
    wait_for(pan.at[pl.ds(0, 8 * LO)], core_send)
    wait_for(best_in.at[pl.ds(0, 6)], best_sem.at[0])
    wait_for(best_in.at[pl.ds(0, 6)], best_sem.at[1])
    for h in range(2):
        top = top_own[:, h * HALF : (h + 1) * HALF]
        for k in range(3):
            top = jnp.maximum(top, best_in[6 + 2 * k + h])
        out_best[:, h * HALF : (h + 1) * HALF] = top


def finish(cent, best, out_cent, out_best):
    out_cent[...] = cent[...]
    out_best[...] = best[...].reshape(NEXT_DEV) / D


def on_device(corpus, row_list, list_slot, member_counts, old_centroids, next_rows):
    vmem = pl.BlockSpec(memory_space=pltpu.VMEM)
    hbm = pl.BlockSpec(memory_space=pl.ANY)
    dma = pltpu.SemaphoreType.DMA
    cent, best = pl.pallas_call(
        kernel,
        out_shape=(
            jax.ShapeDtypeStruct((LO, D), F32),
            jax.ShapeDtypeStruct((1, NEXT_DEV), F32),
        ),
        in_specs=[hbm, vmem, vmem, vmem, vmem, hbm],
        out_specs=(vmem, vmem),
        scratch_shapes=[
            pltpu.VMEM((ROWS_DEV, D), BF16),
            pltpu.VMEM((N_LIST, ROWS_DEV), I32),
            pltpu.VMEM((N_LIST, 128), F32),
            pltpu.VMEM((N_LIST * CAP2, H), BF16),
            pltpu.VMEM((N_LIST, 128), F32),
            pltpu.VMEM((N_LIST * CAP2, H), BF16),
            pltpu.VMEM((N_LIST * CAP, D), BF16),
            pltpu.VMEM((LO, N_LIST * CAP), F32),
            pltpu.VMEM((LO, D), F32),
            pltpu.VMEM((LO, D), BF16),
            pltpu.VMEM((LO, D), BF16),
            pltpu.VMEM((LO, D), BF16),
            pltpu.VMEM((LO, D), BF16),
            pltpu.VMEM((LO, D), F32),
            pltpu.VMEM((ITERS, LO, D), BF16),
            pltpu.VMEM((ITERS - 1, LO, D), BF16),
            pltpu.VMEM((ITERS - 1, LO, D), BF16),
            pltpu.VMEM((LO, 128), F32),
            pltpu.VMEM((N_ROW, 128), F32),
            pltpu.VMEM((LO, 128), F32),
            pltpu.VMEM((SHARDS * LO, D), BF16),
            pltpu.VMEM((NEAR, D), BF16),
            pltpu.VMEM((8, NEAR), F32),
            pltpu.VMEM((12, 1, HALF), F32),
            dma, dma, dma((4,)), dma, dma((4,)),
            dma((2,)), dma((2,)), dma((2 * ITERS,)), dma((2 * ITERS - 2,)), dma((2,)), dma((2,)),
            dma, dma, dma((12,)), dma, dma((4,)), dma, dma((5,)), dma((2,)),
        ],
        compiler_params=pltpu.CompilerParams(
            collective_id=0, has_side_effects=True, vmem_limit_bytes=56 * 2**20
        ),
    )(
        corpus,
        row_list.reshape(1, ROWS_DEV),
        list_slot.reshape(32, 128),
        member_counts.reshape(1, LO),
        old_centroids,
        next_rows,
    )
    return pl.pallas_call(
        finish,
        out_shape=(
            jax.ShapeDtypeStruct((LO, D), F32),
            jax.ShapeDtypeStruct((NEXT_DEV,), F32),
        ),
        in_specs=[vmem, vmem],
        out_specs=(vmem, vmem),
    )(cent, best)


def solution(mesh):
    in_specs = (
        P(("list", "row"), None),
        P(("list", "row")),
        P(),
        P("list"),
        P("list", None),
        P(("list", "row"), None),
    )
    out_specs = (P("list", None), P(("list", "row")))
    return jax.shard_map(
        on_device, mesh=mesh, in_specs=in_specs, out_specs=out_specs, check_vma=False
    )
```
